128 devices in a mesh: passage: 16 (over z, x), span: 8 (over y, core).
Axes of the slice: x: 4, y: 4, z: 4, core: 2. Of those that a mesh axis runs over, the one named last changes fastest.
Arguments:
- velocity: float32 [3, 2048, 2048], P(None, 'passage', 'span'), may hold values from -6 to 6
- viscosity: float32 [2048, 2048], P('passage', 'span'), may hold values from 0.25 to 2
- records: float32 [1048576, 32], P(('passage', 'span')), may hold values from -6 to 6
- owner: int32 [1048576, 1], P(('passage', 'span')), may hold values from 0 to 127; in each aligned block of 8192 rows (0 to 8191, 8192 to 16383, ...) at most 72 rows name the same one
- cell: int32 [1048576], P(('passage', 'span')), may hold values from 0 to 32767
- wall_slot: int32 [1048576], P(('passage', 'span')), may hold values from 0 to 524287
- deposit: float32 [8192, 1024], P(('passage', 'span')), may hold values from 0.05 to 2
Outputs:
- flow_out: float32 [3, 2048, 2048], P(None, 'passage', 'span')
- arrived: float32 [1179648, 32], P(('passage', 'span'))
- deposit_out: float32 [8192, 1024], P(('passage', 'span'))
The draws below stay inside these ranges and needn't reach their ends.
Inputs may be any that keep to these rules, and one draw needn't show every extreme that they name: Among the particles of one device at most 72 have the same owner, and in every draw some owner has exactly 72 particles from some device. Row wall_slot // 1024 of the 512 wall rows of the new owner's span group, place wall_slot % 1024.
All inputs are finite; a program needn't handle non-finite values.
Results may differ from the reference program's by a relative error of at most 0.0003.
Values sent between devices are 32-bit elements; how exact they have to be, the bound alone decides.
No kernel may reach another device: no remote copies, remote signals or barrier semaphores. Data moves between devices by JAX's collectives and lax.ppermute only.
A program may use at most 64 MiB of HBM per device.

```python
import math
import jax
import jax.numpy as jnp
import numpy as np
from jax import lax

CP = 128
CS = 256
P_DEV = 8192
VALUES = 32
SWEEPS = 2
WR = 64
WL = 1024
NP = 2048
NS = 2048
TOTAL = 1048576
CAP = 72
GROUP = 524288
NWR = 8192
N_PASSAGE = 16
N_SPAN = 8
DEVICES = 128


def place_ends(entries, own_key, smallest, high):
    longest = entries.shape.index(max(entries.shape))
    spots = []
    for shift in (0, 1):
        where = [jax.random.randint(jax.random.fold_in(own_key, axis), (), 0, length) for axis, length in enumerate(entries.shape)]
        where[longest] = (where[longest] + shift) % entries.shape[longest]
        spots.append(tuple(where))
    return entries.at[spots[0]].set(smallest).at[spots[1]].set(high)


def levels(stream_key, dims, pieces, least, high):
    loudness, own = 1.0, jax.random.fold_in(stream_key, 6)
    for axis_at, blocks in pieces:
        steps = jnp.exp(jax.random.uniform(jax.random.fold_in(own, axis_at), (blocks,), jnp.float32, least / len(pieces), high / len(pieces)))
        loudness = loudness * jnp.repeat(steps, dims[axis_at] // blocks).reshape([-1 if axis == axis_at else 1 for axis in range(len(dims))])
    return loudness


def deal_out(rng, own, number, rows, amount, top, reach, skew):
    sequence = jax.random.permutation(rng, amount)
    heavy_load, common = portions_of(amount, rows * top, reach, skew, True), portions_of(amount, rows * top, reach, skew, False)
    places = jnp.arange(amount)

    def named(lengths, turn):
        used = int((lengths > 0).sum())
        fixed = max(1, used // 4)
        moved = fixed + (places - fixed + turn * (used - fixed)) % max(1, amount - fixed)
        return jnp.zeros((amount,), jnp.int32).at[sequence[jnp.where(places < fixed, places, moved)]].set(jnp.asarray(lengths, jnp.int32))

    lengths = jnp.where(number % 4 == 0, named(heavy_load, number // 4), named(common, number - number // 4 - 1))
    mixed = jax.random.permutation(jax.random.fold_in(own, 3), amount)
    giver, sink = mixed[0:amount // 2 * 2:2], mixed[1:amount // 2 * 2:2]
    margin = jnp.minimum(lengths[giver] - 1, reach - lengths[sink]) // 2
    margin = jnp.where((giver == sequence[0]) | (sink == sequence[0]) | (lengths[sink] == 0), 0, jnp.maximum(margin, 0))
    moved = jax.random.randint(jax.random.fold_in(own, 4), (amount // 2,), 0, 1 << 20) % (margin + 1)
    lengths = lengths.at[giver].add(-moved).at[sink].add(moved)
    items = jnp.searchsorted(jnp.cumsum(lengths), jnp.arange(rows * top), side="right").astype(jnp.int32)
    listing = items.reshape(top, rows).T
    listing = listing[jax.random.permutation(jax.random.fold_in(own, 1), rows)]
    turn = jax.random.randint(jax.random.fold_in(own, 2), (rows, 1), 0, top)
    return jnp.take_along_axis(listing, (jnp.arange(top)[None, :] + turn) % top, axis=1)


def portions_of(count, total, bound, slope, full):
    loads = [(1 << 20) // math.isqrt(standing ** slope) + 1 for standing in range(1, count + 1)]
    largest = bound if full else min(bound, max(-(-total // count), total * loads[0] // sum(loads)))
    least = 1 if total - largest >= count - 1 else 0
    counts, spare = [largest] + [least] * (count - 1), total - largest - least * (count - 1)
    while spare > 0:
        movable = [i for i in range(1, count) if counts[i] < largest] or [i for i in range(1, count) if counts[i] < bound]
        mass, budget = sum([loads[i] for i in movable]), spare
        for i in movable:
            addition = min(bound - counts[i], max(1, budget * loads[i] // mass), spare)
            counts[i] = counts[i] + addition
            spare = spare - addition
    return np.array(counts)


def gaussian(stream_key, shape, spread, reach, shards=(), kind=jnp.bfloat16):
    factor_of = levels(stream_key, shape, shards, -0.22, 0.18) if shards else 1.0
    values = jax.random.normal(stream_key, shape, jnp.float32) * spread * factor_of
    return jnp.minimum(jnp.maximum(values, -reach), reach).astype(kind)


def setup_inputs(seed: int = 0) -> dict:
    key_of = jax.random.split(jax.random.key(seed), 8)
    velocity = gaussian(key_of[0], (3, NP, NS), 1.0, 6.0, ((1, 16), (2, 8)), jnp.float32)
    viscosity = jnp.clip(jnp.exp(math.log(2.0) - 2.0794415 * jax.random.uniform(key_of[1], (NP, NS), jnp.float32) ** levels(key_of[1], (NP, NS), ((0, 16), (1, 8)), -0.2, 0.2)), 0.25, 2.0)
    records = gaussian(key_of[2], (TOTAL, VALUES), 1.0, 6.0, ((0, 128),), jnp.float32)
    owner_keys = jax.random.split(jax.random.fold_in(key_of[3], 1), TOTAL // P_DEV)
    owner_turns = jax.random.permutation(jax.random.fold_in(key_of[3], 3), TOTAL // P_DEV)
    owner = jax.vmap(lambda own, number: deal_out(jax.random.fold_in(key_of[3], 2), own, number, P_DEV, DEVICES, 1, CAP, 2))(owner_keys, owner_turns).reshape((TOTAL, 1))
    cell = place_ends(jax.random.randint(key_of[4], (TOTAL,), 0, CP * CS), jax.random.fold_in(key_of[4], 1), 0, (CP * CS) - 1).astype(jnp.int32)
    wall_slot = place_ends(jax.random.randint(key_of[5], (TOTAL,), 0, GROUP), jax.random.fold_in(key_of[5], 1), 0, GROUP - 1).astype(jnp.int32)
    deposit = jnp.clip(jnp.exp(math.log(2.0) - 3.6888794 * jax.random.uniform(key_of[6], (NWR, WL), jnp.float32) ** levels(key_of[6], (NWR, WL), ((0, 128),), -0.2, 0.2)), 0.05, 2.0)
    return {"velocity": velocity, "viscosity": viscosity, "records": records, "owner": owner, "cell": cell, "wall_slot": wall_slot, "deposit": deposit}


FLOW_STEP = 0.1
COND_STEP = 0.2
MOVE_STEP = 0.5


def diffuse(padded_rows, viscous):
    center = padded_rows[:, 1:-1, 1:-1]
    mid_nu = viscous[1:-1, 1:-1]
    east_nu = 0.5 * (viscous[1:-1, 2:] + mid_nu)
    west_nu = 0.5 * (viscous[1:-1, :-2] + mid_nu)
    north_nu = 0.5 * (viscous[2:, 1:-1] + mid_nu)
    south_nu = 0.5 * (viscous[:-2, 1:-1] + mid_nu)
    flux_sum = east_nu * (padded_rows[:, 1:-1, 2:] - center) + west_nu * (padded_rows[:, 1:-1, :-2] - center)
    flux_sum = flux_sum + north_nu * (padded_rows[:, 2:, 1:-1] - center) + south_nu * (padded_rows[:, :-2, 1:-1] - center)
    return center + FLOW_STEP * flux_sum


def advance(record_rows, fluid_vel):
    old_vel = record_rows[..., 0:3]
    relax = jax.nn.sigmoid(record_rows[..., 3:4])
    new_vel = old_vel + relax * (fluid_vel - old_vel)
    new_pos = record_rows[..., 6:9] + MOVE_STEP * new_vel
    return jnp.concatenate([new_vel, record_rows[..., 3:6], new_pos, record_rows[..., 9:]], axis=-1)


def pack_rows(record_rows, destination, wall_index, devices, capacity):
    chosen = (destination[:, None] == jnp.arange(devices, dtype=jnp.int32)[None, :]).astype(jnp.int32)
    ranking = jnp.sum(jnp.cumsum(chosen, axis=0) * chosen, axis=1) - 1
    packed_records = jnp.zeros((devices, capacity, record_rows.shape[1]), record_rows.dtype).at[destination, ranking].set(record_rows)
    labels = jnp.zeros((devices, capacity), record_rows.dtype).at[destination, ranking].set(wall_index.astype(record_rows.dtype) + 1.0)
    return packed_records, labels


def capture(arrived_rows, thick):
    arrive_vel = arrived_rows[..., 0:3]
    energy = jnp.sum(arrive_vel * arrive_vel, axis=-1)
    return jax.nn.sigmoid(arrived_rows[..., 4]) * jnp.exp(-thick) * jax.nn.softplus(arrived_rows[..., 5]) * energy / (1.0 + energy)


def conduct(thickness):
    for repeat in range(2):
        widths = [(0, 0)] * (thickness.ndim - 2) + [(1, 1), (1, 1)]
        padded_rows = jnp.pad(thickness, widths, mode="edge")
        beside_all = padded_rows[..., 2:, 1:-1] + padded_rows[..., :-2, 1:-1] + padded_rows[..., 1:-1, 2:] + padded_rows[..., 1:-1, :-2]
        thickness = thickness + COND_STEP * (beside_all - 4.0 * thickness)
    return thickness


def reference(velocity, viscosity, records, owner, cell, wall_slot, deposit):
    flow_field = velocity
    viscous = jnp.pad(viscosity, 1)
    for repeat in range(SWEEPS):
        flow_field = diffuse(jnp.pad(flow_field, ((0, 0), (1, 1), (1, 1))), viscous)
    tile_flow = velocity.reshape(3, N_PASSAGE, CP, N_SPAN, CS).transpose(1, 3, 0, 2, 4).reshape(DEVICES, 3, CP * CS)
    where_at = jnp.broadcast_to(cell.reshape(DEVICES, 1, P_DEV), (DEVICES, 3, P_DEV))
    fluid_vel = jnp.take_along_axis(tile_flow, where_at, axis=2).transpose(0, 2, 1)
    advanced = advance(records.reshape(DEVICES, P_DEV, VALUES), fluid_vel)

    def pack_one(inputs):
        return pack_rows(inputs[0], inputs[1], inputs[2], DEVICES, CAP)

    packed_records, labels = lax.map(pack_one, (advanced, owner.reshape(DEVICES, P_DEV), wall_slot.reshape(DEVICES, P_DEV)))
    arrived = packed_records.transpose(1, 0, 2, 3)
    labels = labels.transpose(1, 0, 2)
    groups = deposit.reshape(N_PASSAGE, GROUP)
    target = labels.astype(jnp.int32) - 1
    wall_index = jnp.maximum(target, 0)
    group_of = jnp.broadcast_to((jnp.arange(DEVICES, dtype=jnp.int32) // N_SPAN)[:, None, None], wall_index.shape)
    gained = jnp.where(target >= 0, capture(arrived, groups[group_of, wall_index]), 0.0)
    increase = jnp.zeros((N_PASSAGE, GROUP), groups.dtype).at[group_of, wall_index].add(gained)
    updated = (groups + increase).reshape(DEVICES, WR, WL)
    return flow_field, arrived.reshape(DEVICES * DEVICES * CAP, VALUES), conduct(updated).reshape(DEVICES * WR, WL)
```

```python
import functools

import jax
import jax.numpy as jnp
from jax import lax
from jax.experimental import pallas as pl
from jax.experimental.pallas import tpu as pltpu
from jax.sharding import PartitionSpec as P

FLOW_STEP = 0.1
COND_STEP = 0.2
MOVE_STEP = 0.5
DEVICES = 128
COUNT = 8192
WIDTH = 32
CAP = 72
HALF = 36
ROWS = 20
LIST = 127
CHUNK = 1024
BLOCK = 256
NT = (((1,), (1,)), ((), ()))
F32 = jnp.float32
BF16 = jnp.bfloat16
I32 = jnp.int32


def iota(shape, dim):
    return lax.broadcasted_iota(I32, shape, dim)


def hot(index, size):
    return (iota((size, index.shape[1]), 0) == index).astype(F32)


def split(x):
    high = x.astype(BF16)
    return high, (x - high.astype(F32)).astype(BF16)


def spread(row, size):
    return jnp.broadcast_to(row, (size, row.shape[1]))


def send_kernel(vel, rec, own, cell, wall, out, aux, table, a_ref, b_ref, a2_ref, b2_ref, acc, acc2, base, mix):
    for c in range(3):
        high, low = split(vel[c].T)
        table[pl.ds(c * 256, 256), 0:128] = high
        table[pl.ds(c * 256, 256), 128:256] = low
    earlier = (iota((BLOCK, BLOCK), 0) < iota((BLOCK, BLOCK), 1)).astype(F32).astype(BF16)
    acc[...] = jnp.zeros_like(acc)
    acc2[...] = jnp.zeros_like(acc2)
    base[...] = jnp.zeros_like(base)

    def chunk(t, carry):
        for b in range(CHUNK // BLOCK):
            lanes = pl.ds(pl.multiple_of(t * CHUNK + b * BLOCK, BLOCK), BLOCK)
            here = pl.ds(b * BLOCK, BLOCK)
            owner = own[0:1, lanes]
            place = cell[0:1, lanes]
            slot = wall[0:1, lanes]
            wall_dev = (owner >> 3) * 8 + (slot >> 16)
            both = jnp.concatenate([hot(owner, 128), hot(wall_dev, 128)], axis=0)
            before = jnp.dot(both.astype(BF16), earlier, preferred_element_type=F32)
            start = base[...]
            picked = both * (before + jnp.concatenate([start, start], axis=1))
            rank = jnp.sum(picked[:128], axis=0, keepdims=True).astype(I32)
            rank2 = jnp.sum(picked[128:], axis=0, keepdims=True).astype(I32)
            base[...] = start + jnp.sum(both, axis=1, keepdims=True)

            row_hot = hot(place >> 8, 128).astype(BF16)
            looked = jnp.dot(table[...], jnp.concatenate([row_hot, row_hot], axis=0), preferred_element_type=F32)
            col_is = iota((256, BLOCK), 0) == (place & 255)
            fluid = jnp.concatenate(
                [
                    jnp.sum(jnp.where(col_is, looked[c * 256 : (c + 1) * 256], 0.0), axis=0, keepdims=True)
                    for c in range(3)
                ],
                axis=0,
            )
            r = rec[:, lanes]
            old = r[0:3]
            new = old + jax.nn.sigmoid(r[3:4]) * (fluid - old)
            values = jnp.concatenate([new, r[3:6], r[6:9] + MOVE_STEP * new, r[9:]], axis=0)
            energy = jnp.sum(new * new, axis=0, keepdims=True)
            mass = r[5:6]
            soft = jnp.maximum(mass, 0.0) + jnp.log1p(jnp.exp(-jnp.abs(mass)))
            amount = jax.nn.sigmoid(r[4:5]) * soft * energy / (1.0 + energy)
            wall_row = (slot >> 10) & 63
            first = ((slot >> 8) & 3) * 64 + wall_row
            second = slot & 255
            aux[0:1, lanes] = amount
            aux[1:2, lanes] = (first * 256 + second).astype(F32)
            aux[2:3, lanes] = wall_dev.astype(F32)
            aux[3:4, lanes] = rank2.astype(F32)

            late = (rank >= HALF).astype(I32)
            step = rank - HALF * late
            b_ref[:, here] = hot(owner + 128 * late, 256).astype(BF16)
            main = hot(step, 32).astype(BF16)
            parts = split(values)
            for part in range(2):
                for f in range(WIDTH):
                    row = ((part * 9 + f % 8) * 4 + f // 8) * 32
                    a_ref[pl.ds(row, 32), here] = main * spread(parts[part][f : f + 1], 32)
                for e in range(4):
                    a_ref[pl.ds(((part * 9 + 8) * 4 + e) * 32, 32), here] = (
                        (step == 32 + e).astype(F32).astype(BF16) * parts[part]
                    )
            late2 = (rank2 >= 64).astype(I32)
            step2 = jnp.where(rank2 < LIST, rank2 - 64 * late2, 64)
            b2_ref[:, here] = hot(wall_dev + 128 * late2, 256).astype(BF16)
            main2 = hot(step2, 64).astype(BF16)
            a_high, a_low = split(amount)
            for v, x in enumerate((first.astype(F32).astype(BF16), second.astype(F32).astype(BF16), a_high, a_low)):
                a2_ref[pl.ds(v * 64, 64), here] = main2 * spread(x, 64)
        acc[...] += lax.dot_general(a_ref[...], b_ref[...], NT, preferred_element_type=F32)
        acc2[...] += lax.dot_general(a2_ref[...], b2_ref[...], NT, preferred_element_type=F32)
        return carry

    lax.fori_loop(0, COUNT // CHUNK, chunk, 0)

    for c in range(9):
        both = acc[pl.ds(c * 128, 128), :] + acc[pl.ds((9 + c) * 128, 128), :]
        if c == 8:
            for h in range(2):
                mix[h] = both[:, h * 128 : (h + 1) * 128]
                for f in range(WIDTH):
                    mix[2 + h, 4 * (31 - f) : 4 * (31 - f) + 4, :] = mix[h, pl.ds(f, 4, stride=32), :]
        for h in range(2):
            mine = both[:, h * 128 : (h + 1) * 128] if c < 8 else mix[2 + h]
            out[pl.ds(h * 8 + c if c < 8 else 16 + h, 128, stride=ROWS), :] = mine.T
    spot = acc2[0:64, :] * 256.0 + acc2[64:128, :]
    amount = acc2[128:192, :] + acc2[192:256, :]
    spot = jnp.concatenate([spot[:, :128], spot[:, 128:]], axis=0).T
    amount = jnp.concatenate([amount[:, :128], amount[:, 128:]], axis=0).T
    most = jnp.max(base[128:, :])
    out[pl.ds(18, 128, stride=ROWS), :] = jnp.where(iota((128, 128), 1) == LIST, most, spot)
    out[pl.ds(19, 128, stride=ROWS), :] = amount


def send(velocity, records_t, owner, cell, wall_slot, interpret=False):
    return pl.pallas_call(
        send_kernel,
        out_shape=(
            jax.ShapeDtypeStruct((DEVICES * ROWS, 128), F32),
            jax.ShapeDtypeStruct((4, COUNT), F32),
        ),
        in_specs=[pl.BlockSpec(memory_space=pltpu.VMEM)] * 5,
        out_specs=[pl.BlockSpec(memory_space=pltpu.VMEM)] * 2,
        scratch_shapes=[
            pltpu.VMEM((768, 256), BF16),
            pltpu.VMEM((2304, CHUNK), BF16),
            pltpu.VMEM((256, CHUNK), BF16),
            pltpu.VMEM((256, CHUNK), BF16),
            pltpu.VMEM((256, CHUNK), BF16),
            pltpu.VMEM((2304, 256), F32),
            pltpu.VMEM((256, 256), F32),
            pltpu.VMEM((256, 128), F32),
            pltpu.VMEM((4, 128, 128), F32),
        ],
        compiler_params=pltpu.CompilerParams(vmem_limit_bytes=48 << 20),
        name="send",
    )(velocity, records_t, owner, cell, wall_slot)


def conduct(t):
    rows = iota(t.shape, 0)
    cols = iota(t.shape, 1)
    for repeat in range(2):
        up = jnp.where(rows == 0, t, pltpu.roll(t, 1, 0))
        down = jnp.where(rows == t.shape[0] - 1, t, pltpu.roll(t, t.shape[0] - 1, 0))
        left = jnp.where(cols == 0, t, pltpu.roll(t, 1, 1))
        right = jnp.where(cols == t.shape[1] - 1, t, pltpu.roll(t, t.shape[1] - 1, 1))
        t = t + COND_STEP * ((down + up + right + left) - 4.0 * t)
    return t


def receive_kernel(got, deposit, arrived, deposit_out, total, most, h1_ref, h2_ref, acc):
    lane = iota((8, 128), 1)

    def unpack(g, carry):
        tiles = [[None] * 9 for _ in range(4)]
        for s in range(16):
            row = g * (16 * ROWS) + s * ROWS
            for h in range(2):
                body = got[pl.ds(row + 8 * h, 8), :]
                rest = jnp.broadcast_to(got[pl.ds(row + 16 + h, 1), :], (8, 128))
                rest = pltpu.roll(rest, 0, 1, stride=4, stride_axis=0)
                at = s * CAP + h * HALF
                for k in range(4):
                    for piece, to, size in (
                        (pltpu.roll(body, (at - 32 * k) % 128, 1), at, 32),
                        (pltpu.roll(rest, (at + 32 - 124 + 32 * k) % 128, 1), at + 32, 4),
                    ):
                        tile, off = to // 128, to % 128
                        had = tiles[k][tile]
                        tiles[k][tile] = piece if off == 0 or had is None else jnp.where(lane >= off, piece, had)
                        if off + size > 128:
                            tiles[k][tile + 1] = piece
        for k in range(4):
            for i in range(9):
                arrived[8 * k : 8 * k + 8, pl.ds(pl.multiple_of(g * 1152 + i * 128, 128), 128)] = tiles[k][i]
        return carry

    lax.fori_loop(0, 8, unpack, 0)

    acc[...] = jnp.zeros_like(acc)

    def strike(g, carry):
        spot8 = got[pl.ds(g * (8 * ROWS) + 18, 8, stride=ROWS), :].astype(I32)
        amount8 = got[pl.ds(g * (8 * ROWS) + 19, 8, stride=ROWS), :]
        for s in range(8):
            here = pl.ds(s * 128, 128)
            spot = spot8[s : s + 1]
            h1_ref[:, here] = hot(spot >> 8, 256).astype(BF16)
            second = hot(spot & 255, 256).astype(BF16)
            for part, x in enumerate(split(amount8[s : s + 1])):
                h2_ref[pl.ds(part * 256, 256), here] = second * spread(x, 256)
        acc[...] += lax.dot_general(h1_ref[...], h2_ref[...], NT, preferred_element_type=F32)
        return carry

    lax.fori_loop(0, DEVICES // 8, strike, 0)
    struck = acc[:, 0:256] + acc[:, 256:512]
    struck = jnp.concatenate([struck[64 * c : 64 * c + 64] for c in range(4)], axis=1)
    total[...] = struck
    had = deposit[...]
    deposit_out[...] = conduct(had + jnp.exp(-had) * struck)
    counts = got[pl.ds(18, DEVICES, stride=ROWS), :]
    most[...] = jnp.max(counts[:, LIST:], axis=0, keepdims=True).reshape(1, 1)


def receive(got, deposit):
    return pl.pallas_call(
        receive_kernel,
        out_shape=(
            jax.ShapeDtypeStruct((WIDTH, DEVICES * CAP), F32),
            jax.ShapeDtypeStruct((64, 1024), F32),
            jax.ShapeDtypeStruct((64, 1024), F32),
            jax.ShapeDtypeStruct((1, 1), F32),
        ),
        in_specs=[pl.BlockSpec(memory_space=pltpu.VMEM)] * 2,
        out_specs=[pl.BlockSpec(memory_space=pltpu.VMEM)] * 4,
        scratch_shapes=[
            pltpu.VMEM((256, 1024), BF16),
            pltpu.VMEM((512, 1024), BF16),
            pltpu.VMEM((256, 512), F32),
        ],
        compiler_params=pltpu.CompilerParams(vmem_limit_bytes=48 << 20),
        name="receive",
    )(got, deposit)


def shifted(cells, axis, up):
    count = lax.axis_size(axis)
    pairs = [(i, i + 1) if up else (i + 1, i) for i in range(count - 1)]
    return lax.ppermute(cells, axis, pairs)


def flow(velocity, viscosity):
    fields = jnp.concatenate([velocity, viscosity[None]], axis=0)
    north = shifted(fields[:, -2:, :].reshape(8, -1), "passage", True).reshape(4, 2, -1)
    south = shifted(fields[:, :2, :].reshape(8, -1), "passage", False).reshape(4, 2, -1)
    tall = jnp.concatenate([north, fields, south], axis=1)
    high = tall.shape[1]
    edge = lambda x: x.transpose(0, 2, 1).reshape(8, high)
    back = lambda x: x.reshape(4, 2, high).transpose(0, 2, 1)
    west = back(shifted(edge(tall[:, :, -2:]), "span", True))
    east = back(shifted(edge(tall[:, :, :2]), "span", False))
    wide = jnp.concatenate([west, tall, east], axis=2)
    f, nu = wide[:3], wide[3]
    first = diffuse(f, nu)
    rows = jnp.arange(first.shape[1])[:, None]
    cols = jnp.arange(first.shape[2])[None, :]
    pi, si = lax.axis_index("passage"), lax.axis_index("span")
    outside = (
        ((rows == 0) & (pi == 0))
        | ((rows == first.shape[1] - 1) & (pi == lax.axis_size("passage") - 1))
        | ((cols == 0) & (si == 0))
        | ((cols == first.shape[2] - 1) & (si == lax.axis_size("span") - 1))
    )
    first = jnp.where(outside[None], 0.0, first)
    return diffuse(first, nu[1:-1, 1:-1])


def diffuse(padded_rows, viscous):
    center = padded_rows[:, 1:-1, 1:-1]
    mid_nu = viscous[1:-1, 1:-1]
    east_nu = 0.5 * (viscous[1:-1, 2:] + mid_nu)
    west_nu = 0.5 * (viscous[1:-1, :-2] + mid_nu)
    north_nu = 0.5 * (viscous[2:, 1:-1] + mid_nu)
    south_nu = 0.5 * (viscous[:-2, 1:-1] + mid_nu)
    flux_sum = east_nu * (padded_rows[:, 1:-1, 2:] - center) + west_nu * (padded_rows[:, 1:-1, :-2] - center)
    flux_sum = (
        flux_sum
        + north_nu * (padded_rows[:, 2:, 1:-1] - center)
        + south_nu * (padded_rows[:, :-2, 1:-1] - center)
    )
    return center + FLOW_STEP * flux_sum


def conduct_plain(thickness):
    for repeat in range(2):
        padded = jnp.pad(thickness, 1, mode="edge")
        beside = padded[2:, 1:-1] + padded[:-2, 1:-1] + padded[1:-1, 2:] + padded[1:-1, :-2]
        thickness = thickness + COND_STEP * (beside - 4.0 * thickness)
    return thickness


def rest_of_lists(total, most, aux, deposit):
    amount, spot, wall_dev, rank = aux[0], aux[1], aux[2].astype(I32), aux[3].astype(I32)

    def one_round(state):
        turn, total = state
        low = turn * LIST
        taken = (rank >= low) & (rank < low + LIST)
        index = jnp.where(taken, wall_dev * 128 + rank - low, DEVICES * 128)
        lists = jnp.zeros((DEVICES * 128, 2), F32)
        lists = lists.at[index].set(jnp.stack([amount, spot], axis=1), mode="drop")
        lists = lists.reshape(DEVICES, 128, 2).transpose(0, 2, 1).reshape(DEVICES, 1, 256)
        lists = lax.all_to_all(lists, ("passage", "span"), 0, 0, tiled=True).reshape(DEVICES, 2, 128)
        code = lists[:, 1].reshape(-1).astype(I32)
        first, second = code >> 8, code & 255
        place = (first & 63) * 1024 + (first >> 6) * 256 + second
        added = jnp.zeros((64 * 1024,), F32).at[place].add(lists[:, 0].reshape(-1))
        return turn + 1, total + added.reshape(64, 1024)

    total = lax.while_loop(lambda state: state[0] * LIST < most.astype(I32), one_round, (1, total))[1]
    return conduct_plain(deposit + jnp.exp(-deposit) * total)


def local(velocity, viscosity, records, owner, cell, wall_slot, deposit):
    packed, aux = send(
        velocity, records.T, owner.reshape(1, COUNT), cell.reshape(1, COUNT), wall_slot.reshape(1, COUNT)
    )
    got = lax.all_to_all(packed.reshape(DEVICES, 1, ROWS * 128), ("passage", "span"), 0, 0, tiled=True)
    flow_out = flow(velocity, viscosity)
    arrived, deposit_out, total, most = receive(got.reshape(DEVICES * ROWS, 128), deposit)
    most = most[0, 0]
    deposit_out = lax.cond(
        most > LIST, lambda: rest_of_lists(total, most, aux, deposit), lambda: deposit_out
    )
    return flow_out, arrived.T, deposit_out


def solution(mesh):
    each = ("passage", "span")
    tile = P(None, "passage", "span")
    rows = P(each, None)
    return jax.shard_map(
        local,
        mesh=mesh,
        in_specs=(tile, P("passage", "span"), rows, rows, P(each), P(each), rows),
        out_specs=(tile, rows, rows),
        check_vma=False,
    )
```

```python
import functools

import jax
import jax.numpy as jnp
from jax import lax
from jax.experimental import pallas as pl
from jax.experimental.pallas import tpu as pltpu
from jax.sharding import PartitionSpec as P

FLOW_STEP = 0.1
COND_STEP = 0.2
MOVE_STEP = 0.5
DEVICES = 128
COUNT = 8192
WIDTH = 32
CAP = 72
HALF = 36
ROWS = 20
LIST = 127
CHUNK = 1024
MORE = COUNT + CHUNK
BLOCK = 256
NT = (((1,), (1,)), ((), ()))
F32 = jnp.float32
BF16 = jnp.bfloat16
I32 = jnp.int32


def iota(shape, dim):
    return lax.broadcasted_iota(I32, shape, dim)


def hot(index, size):
    return (iota((size, index.shape[1]), 0) == index).astype(F32)


def split(x):
    high = x.astype(BF16)
    return high, (x - high.astype(F32)).astype(BF16)


def spread(row, size):
    return jnp.broadcast_to(row, (size, row.shape[1]))


def counting(size, lanes):
    return iota((size, lanes), 0).astype(F32).astype(BF16)


def ones_at(row, size):
    here = counting(size, row.shape[1]) == jnp.broadcast_to(row.astype(BF16), (size, row.shape[1]))
    return jnp.where(here, jnp.ones(here.shape, BF16), jnp.zeros(here.shape, BF16))


def send_kernel(
    vel_h, rec_h, own_h, cell_h, wall_h, out, aux,
    vel, rec, own, cell, wall, table, val, meta, a_ref, b_ref, a2_ref, b2_ref, acc, acc2, base, mix, sems,
):
    copies = [
        pltpu.make_async_copy(source, target, sems.at[i])
        for i, (source, target) in enumerate(
            ((vel_h, vel), (own_h, own.at[:, :COUNT]), (cell_h, cell.at[:, :COUNT]), (wall_h, wall.at[:, :COUNT]), (rec_h, rec.at[:, :COUNT]))
        )
    ]
    for copy in copies:
        copy.start()
    acc[...] = jnp.zeros_like(acc)
    acc2[...] = jnp.zeros_like(acc2)
    base[...] = jnp.zeros_like(base)
    earlier = (iota((BLOCK, BLOCK), 0) < iota((BLOCK, BLOCK), 1)).astype(F32).astype(BF16)
    past = pl.ds(COUNT, CHUNK)
    own[:, past] = jnp.full((1, CHUNK), 128, I32)
    cell[:, past] = jnp.zeros((1, CHUNK), I32)
    wall[:, past] = jnp.zeros((1, CHUNK), I32)
    rec[:, past] = jnp.zeros((WIDTH, CHUNK), F32)
    copies[0].wait()
    for c in range(3):
        high, low = split(vel[c].T)
        table[pl.ds(c * 256, 256), 0:128] = high
        table[pl.ds(c * 256, 256), 128:256] = low
    for copy in copies[1:]:
        copy.wait()

    def prepare(i):
        if True:
            lanes = pl.ds(pl.multiple_of(i * BLOCK, BLOCK), BLOCK)
            owner = own[0:1, lanes]
            place = cell[0:1, lanes]
            slot = wall[0:1, lanes]
            wall_dev = (owner >> 3) * 8 + (slot >> 16)
            both = jnp.concatenate([ones_at(owner.astype(F32), 128), ones_at(wall_dev.astype(F32), 128)], axis=0)
            before = jnp.dot(both, earlier, preferred_element_type=F32)
            both = both.astype(F32)
            start = base[...]
            picked = both * (before + jnp.concatenate([start, start], axis=1))
            rank = jnp.sum(picked[:128], axis=0, keepdims=True)
            rank2 = jnp.sum(picked[128:], axis=0, keepdims=True)
            base[...] = start + jnp.sum(both, axis=1, keepdims=True)

            row_hot = ones_at((place >> 8).astype(F32), 128)
            looked = jnp.dot(table[...], jnp.concatenate([row_hot, row_hot], axis=0), preferred_element_type=F32)
            col_is = iota((256, BLOCK), 0) == (place & 255)
            fluid = jnp.concatenate(
                [
                    jnp.sum(jnp.where(col_is, looked[c * 256 : (c + 1) * 256], 0.0), axis=0, keepdims=True)
                    for c in range(3)
                ],
                axis=0,
            )
            r = rec[:, lanes]
            old = r[0:3]
            new = old + jax.nn.sigmoid(r[3:4]) * (fluid - old)
            values = jnp.concatenate([new, r[3:6], r[6:9] + MOVE_STEP * new, r[9:]], axis=0)
            energy = jnp.sum(new * new, axis=0, keepdims=True)
            mass = r[5:6]
            soft = jnp.maximum(mass, 0.0) + jnp.log1p(jnp.exp(-jnp.abs(mass)))
            amount = jax.nn.sigmoid(r[4:5]) * soft * energy / (1.0 + energy)
            first = ((slot >> 8) & 3) * 64 + ((slot >> 10) & 63)
            second = slot & 255
            aux[0:1, lanes] = amount
            aux[1:2, lanes] = (first * 256 + second).astype(F32)
            aux[2:3, lanes] = wall_dev.astype(F32)
            aux[3:4, lanes] = rank2

            highs = values.astype(BF16).astype(F32)
            val[0:32, lanes] = highs
            val[32:64, lanes] = values - highs
            late = rank >= HALF
            late2 = rank2 >= 64.0
            high = amount.astype(BF16).astype(F32)
            meta[0:1, lanes] = jnp.where(late, rank - HALF, rank)
            meta[1:2, lanes] = owner.astype(F32) + jnp.where(late, 128.0, 0.0)
            meta[2:3, lanes] = jnp.where(rank2 < LIST, jnp.where(late2, rank2 - 64.0, rank2), 64.0)
            meta[3:4, lanes] = wall_dev.astype(F32) + jnp.where(late2, 128.0, 0.0)
            meta[4:5, lanes] = first.astype(F32)
            meta[5:6, lanes] = second.astype(F32)
            meta[6:7, lanes] = high
            meta[7:8, lanes] = amount - high

    def place_values(t):
        lanes = pl.ds(pl.multiple_of(t * CHUNK, CHUNK), CHUNK)
        row = lambda ref, i, size: jnp.broadcast_to(ref[i : i + 1, lanes].astype(BF16), (size, CHUNK))
        step = row(meta, 0, 32)
        zero = jnp.zeros((32, CHUNK), BF16)
        main = counting(32, CHUNK) == step
        b_ref[...] = ones_at(meta[1:2, lanes], 256)
        for part in range(2):
            for f in range(WIDTH):
                to = ((part * 9 + f % 8) * 4 + f // 8) * 32
                a_ref[pl.ds(to, 32), :] = jnp.where(main, row(val, part * 32 + f, 32), zero)
            whole = val[part * 32 : part * 32 + 32, lanes].astype(BF16)
            for e in range(4):
                to = ((part * 9 + 8) * 4 + e) * 32
                a_ref[pl.ds(to, 32), :] = jnp.where(step == 32 + e, whole, zero)
        main2 = counting(64, CHUNK) == row(meta, 2, 64)
        zero = jnp.zeros((64, CHUNK), BF16)
        b2_ref[...] = ones_at(meta[3:4, lanes], 256)
        for v in range(4):
            a2_ref[pl.ds(v * 64, 64), :] = jnp.where(main2, row(meta, 4 + v, 64), zero)

    pieces = CHUNK // BLOCK
    rows = 2304 // pieces

    def add(piece):
        some = pl.ds(piece * rows, rows)
        acc[some, :] += lax.dot_general(a_ref[some, :], b_ref[...], NT, preferred_element_type=F32)

    def first_blocks(i, carry):
        prepare(i)
        return carry

    lax.fori_loop(0, pieces, first_blocks, 0)

    def chunk(t, carry):
        place_values(t)
        acc2[...] += lax.dot_general(a2_ref[...], b2_ref[...], NT, preferred_element_type=F32)
        for piece in range(pieces):
            add(piece)
            prepare((t + 1) * pieces + piece)
        return carry

    lax.fori_loop(0, COUNT // CHUNK, chunk, 0)

    def summed(c):
        low = pl.multiple_of(c * 128, 128)
        return acc[pl.ds(low, 128), :] + acc[pl.ds(1152 + low, 128), :]

    def main_rows(c, carry):
        both = summed(c)
        for h in range(2):
            out[pl.ds(h * 8 + c, 128, stride=ROWS), :] = both[:, h * 128 : (h + 1) * 128].T
        return carry

    lax.fori_loop(0, 8, main_rows, 0)
    rest = summed(8)
    for h in range(2):
        mix[h] = rest[:, h * 128 : (h + 1) * 128]
    for f in range(WIDTH):
        to = 4 * (f // 8 * 8 + 7 - f % 8)
        for h in range(2):
            mix[2 + h, to : to + 4, :] = mix[h, pl.ds(f, 4, stride=32), :]
    for h in range(2):
        out[pl.ds(16 + h, 128, stride=ROWS), :] = mix[2 + h].T
    spot = acc2[0:64, :] * 256.0 + acc2[64:128, :]
    amount = acc2[128:192, :] + acc2[192:256, :]
    spot = jnp.concatenate([spot[:, :128], spot[:, 128:]], axis=0).T
    amount = jnp.concatenate([amount[:, :128], amount[:, 128:]], axis=0).T
    most = jnp.max(base[128:, :])
    out[pl.ds(18, 128, stride=ROWS), :] = jnp.where(iota((128, 128), 1) == LIST, most, spot)
    out[pl.ds(19, 128, stride=ROWS), :] = amount


def send(velocity, records_t, owner, cell, wall_slot):
    return pl.pallas_call(
        send_kernel,
        out_shape=(
            jax.ShapeDtypeStruct((DEVICES * ROWS, 128), F32),
            jax.ShapeDtypeStruct((4, MORE), F32),
        ),
        in_specs=[pl.BlockSpec(memory_space=pl.ANY)] * 5,
        out_specs=[pl.BlockSpec(memory_space=pltpu.VMEM)] * 2,
        scratch_shapes=[
            pltpu.VMEM((3, 128, 256), F32),
            pltpu.VMEM((WIDTH, MORE), F32),
            pltpu.VMEM((1, MORE), I32),
            pltpu.VMEM((1, MORE), I32),
            pltpu.VMEM((1, MORE), I32),
            pltpu.VMEM((768, 256), BF16),
            pltpu.VMEM((64, MORE), F32),
            pltpu.VMEM((8, MORE), F32),
            pltpu.VMEM((2304, CHUNK), BF16),
            pltpu.VMEM((256, CHUNK), BF16),
            pltpu.VMEM((256, CHUNK), BF16),
            pltpu.VMEM((256, CHUNK), BF16),
            pltpu.VMEM((2304, 256), F32),
            pltpu.VMEM((256, 256), F32),
            pltpu.VMEM((256, 128), F32),
            pltpu.VMEM((4, 128, 128), F32),
            pltpu.SemaphoreType.DMA((5,)),
        ],
        compiler_params=pltpu.CompilerParams(vmem_limit_bytes=56 << 20),
        name="send",
    )(velocity, records_t, owner, cell, wall_slot)


def conduct(t):
    rows = iota(t.shape, 0)
    cols = iota(t.shape, 1)
    for repeat in range(2):
        up = jnp.where(rows == 0, t, pltpu.roll(t, 1, 0))
        down = jnp.where(rows == t.shape[0] - 1, t, pltpu.roll(t, t.shape[0] - 1, 0))
        left = jnp.where(cols == 0, t, pltpu.roll(t, 1, 1))
        right = jnp.where(cols == t.shape[1] - 1, t, pltpu.roll(t, t.shape[1] - 1, 1))
        t = t + COND_STEP * ((down + up + right + left) - 4.0 * t)
    return t


def receive_kernel(got, deposit, arrived, deposit_out, total, most, h1_ref, h2_ref, acc):
    lane = iota((8, 128), 1)
    wide = iota((64, 128), 1)
    even = ((wide >= 32) & (wide < 36)) | ((wide >= 96) & (wide < 100))
    odd = ((wide >= 64) & (wide < 68)) | (wide < 4)
    upto = iota((256, 128), 0).astype(F32).astype(BF16)

    groups = DEVICES // 16

    def stack(row):
        return jnp.concatenate([got[pl.ds(row + g * (16 * ROWS), 8), :] for g in range(groups)], axis=0)

    def fan(row):
        one = [got[pl.ds(row + g * (16 * ROWS), 1), :] for g in range(groups)]
        return jnp.concatenate(
            [pltpu.roll(jnp.broadcast_to(x, (8, 128)), 4, 1, stride=4, stride_axis=0) for x in one], axis=0
        )

    def unpack(s, carry):
        at = s * CAP
        tile, off = at >> 7, at & 127
        halves = []
        for h in range(2):
            body = stack(s * ROWS + 8 * h)
            rest = fan(s * ROWS + 16 + h)
            halves.append((jnp.where(even, rest, body), jnp.where(odd, rest, body)))
        for k in range(4):
            last = pltpu.roll(halves[1][k % 2], HALF, 1)
            piece = jnp.where((wide >= 32 * k) & (wide < 32 * k + HALF) | (wide < 32 * k + HALF - 128), halves[0][k % 2], last)
            piece = pltpu.roll(piece, (at - 32 * k) & 127, 1)
            over = off + CAP > 128
            for g in range(groups):
                mine = piece[8 * g : 8 * g + 8]
                to = pl.ds(pl.multiple_of((g * 9 + tile) * 128, 128), 128)
                made = jnp.where(lane >= off, mine, arrived[8 * k : 8 * k + 8, to])
                arrived[8 * k : 8 * k + 8, to] = made
                to = pl.ds(pl.multiple_of((g * 9 + tile + over.astype(I32)) * 128, 128), 128)
                arrived[8 * k : 8 * k + 8, to] = jnp.where(over, mine, made)
        return carry

    def build(g, slot):
        spot16 = got[pl.ds(g * (16 * ROWS) + 18, 16, stride=ROWS), :].astype(I32)
        amount16 = got[pl.ds(g * (16 * ROWS) + 19, 16, stride=ROWS), :]
        firsts = (spot16 >> 8).astype(F32)
        seconds = (spot16 & 255).astype(F32)
        highs = amount16.astype(BF16).astype(F32)
        lows = amount16 - highs
        one = jnp.ones((256, 128), BF16)
        zero = jnp.zeros((256, 128), BF16)
        for s in range(16):
            here = pl.ds(s * 128, 128)
            row = lambda x: jnp.broadcast_to(x[s : s + 1].astype(BF16), (256, 128))
            h1_ref[slot, :, here] = jnp.where(upto == row(firsts), one, zero)
            same = upto == row(seconds)
            h2_ref[slot, 0:256, here] = jnp.where(same, row(highs), zero)
            h2_ref[slot, 256:512, here] = jnp.where(same, row(lows), zero)

    def add(slot):
        acc[...] += lax.dot_general(h1_ref[slot], h2_ref[slot], NT, preferred_element_type=F32)

    acc[...] = jnp.zeros_like(acc)
    build(0, 0)

    def pair_of_groups(u, carry):
        unpack(4 * u, 0)
        build(2 * u + 1, 1)
        unpack(4 * u + 1, 0)
        add(0)
        unpack(4 * u + 2, 0)
        build(jnp.minimum(2 * u + 2, 7), 0)
        unpack(4 * u + 3, 0)
        add(1)
        return carry

    lax.fori_loop(0, 4, pair_of_groups, 0)
    struck = acc[:, 0:256] + acc[:, 256:512]
    struck = jnp.concatenate([struck[64 * c : 64 * c + 64] for c in range(4)], axis=1)
    total[...] = struck
    had = deposit[...]
    deposit_out[...] = conduct(had + jnp.exp(-had) * struck)
    counts = got[pl.ds(18, DEVICES, stride=ROWS), :]
    most[...] = jnp.max(counts[:, LIST:], axis=0, keepdims=True).reshape(1, 1)


def receive(got, deposit):
    return pl.pallas_call(
        receive_kernel,
        out_shape=(
            jax.ShapeDtypeStruct((WIDTH, DEVICES * CAP), F32),
            jax.ShapeDtypeStruct((64, 1024), F32),
            jax.ShapeDtypeStruct((64, 1024), F32),
            jax.ShapeDtypeStruct((1, 1), F32),
        ),
        in_specs=[pl.BlockSpec(memory_space=pltpu.VMEM)] * 2,
        out_specs=[pl.BlockSpec(memory_space=pltpu.VMEM)] * 4,
        scratch_shapes=[
            pltpu.VMEM((2, 256, 2048), BF16),
            pltpu.VMEM((2, 512, 2048), BF16),
            pltpu.VMEM((256, 512), F32),
        ],
        compiler_params=pltpu.CompilerParams(vmem_limit_bytes=48 << 20),
        name="receive",
    )(got, deposit)


def shifted(cells, axis, up):
    count = lax.axis_size(axis)
    pairs = [(i, i + 1) if up else (i + 1, i) for i in range(count - 1)]
    return lax.ppermute(cells, axis, pairs)


def flow(velocity, viscosity):
    fields = jnp.concatenate([velocity, viscosity[None]], axis=0)
    north = shifted(fields[:, -2:, :].reshape(8, -1), "passage", True).reshape(4, 2, -1)
    south = shifted(fields[:, :2, :].reshape(8, -1), "passage", False).reshape(4, 2, -1)
    tall = jnp.concatenate([north, fields, south], axis=1)
    high = tall.shape[1]
    edge = lambda x: x.transpose(0, 2, 1).reshape(8, high)
    back = lambda x: x.reshape(4, 2, high).transpose(0, 2, 1)
    west = back(shifted(edge(tall[:, :, -2:]), "span", True))
    east = back(shifted(edge(tall[:, :, :2]), "span", False))
    wide = jnp.concatenate([west, tall, east], axis=2)
    f, nu = wide[:3], wide[3]
    first = diffuse(f, nu)
    rows = jnp.arange(first.shape[1])[:, None]
    cols = jnp.arange(first.shape[2])[None, :]
    pi, si = lax.axis_index("passage"), lax.axis_index("span")
    outside = (
        ((rows == 0) & (pi == 0))
        | ((rows == first.shape[1] - 1) & (pi == lax.axis_size("passage") - 1))
        | ((cols == 0) & (si == 0))
        | ((cols == first.shape[2] - 1) & (si == lax.axis_size("span") - 1))
    )
    first = jnp.where(outside[None], 0.0, first)
    return diffuse(first, nu[1:-1, 1:-1])


def diffuse(padded_rows, viscous):
    center = padded_rows[:, 1:-1, 1:-1]
    mid_nu = viscous[1:-1, 1:-1]
    east_nu = 0.5 * (viscous[1:-1, 2:] + mid_nu)
    west_nu = 0.5 * (viscous[1:-1, :-2] + mid_nu)
    north_nu = 0.5 * (viscous[2:, 1:-1] + mid_nu)
    south_nu = 0.5 * (viscous[:-2, 1:-1] + mid_nu)
    flux_sum = east_nu * (padded_rows[:, 1:-1, 2:] - center) + west_nu * (padded_rows[:, 1:-1, :-2] - center)
    flux_sum = (
        flux_sum
        + north_nu * (padded_rows[:, 2:, 1:-1] - center)
        + south_nu * (padded_rows[:, :-2, 1:-1] - center)
    )
    return center + FLOW_STEP * flux_sum


def conduct_plain(thickness):
    for repeat in range(2):
        padded = jnp.pad(thickness, 1, mode="edge")
        beside = padded[2:, 1:-1] + padded[:-2, 1:-1] + padded[1:-1, 2:] + padded[1:-1, :-2]
        thickness = thickness + COND_STEP * (beside - 4.0 * thickness)
    return thickness


def rest_of_lists(total, most, aux, deposit):
    amount, spot = aux[0, :COUNT], aux[1, :COUNT]
    wall_dev, rank = aux[2, :COUNT].astype(I32), aux[3, :COUNT].astype(I32)

    def one_round(state):
        turn, total = state
        low = turn * LIST
        taken = (rank >= low) & (rank < low + LIST)
        index = jnp.where(taken, wall_dev * 128 + rank - low, DEVICES * 128)
        lists = jnp.zeros((DEVICES * 128, 2), F32)
        lists = lists.at[index].set(jnp.stack([amount, spot], axis=1), mode="drop")
        lists = lists.reshape(DEVICES, 128, 2).transpose(0, 2, 1).reshape(DEVICES, 1, 256)
        lists = lax.all_to_all(lists, ("passage", "span"), 0, 0, tiled=True).reshape(DEVICES, 2, 128)
        code = lists[:, 1].reshape(-1).astype(I32)
        first, second = code >> 8, code & 255
        place = (first & 63) * 1024 + (first >> 6) * 256 + second
        added = jnp.zeros((64 * 1024,), F32).at[place].add(lists[:, 0].reshape(-1))
        return turn + 1, total + added.reshape(64, 1024)

    total = lax.while_loop(lambda state: state[0] * LIST < most.astype(I32), one_round, (1, total))[1]
    return conduct_plain(deposit + jnp.exp(-deposit) * total)


def local(velocity, viscosity, records, owner, cell, wall_slot, deposit):
    packed, aux = send(
        velocity, records.T, owner.reshape(1, COUNT), cell.reshape(1, COUNT), wall_slot.reshape(1, COUNT)
    )
    packed, velocity, viscosity = lax.optimization_barrier((packed, velocity, viscosity))
    got = lax.all_to_all(packed.reshape(DEVICES, 1, ROWS * 128), ("passage", "span"), 0, 0, tiled=True)
    flow_out = flow(velocity, viscosity)
    arrived, deposit_out, total, most = receive(got.reshape(DEVICES * ROWS, 128), deposit)
    most = most[0, 0]
    deposit_out = lax.cond(
        most > LIST, lambda: rest_of_lists(total, most, aux, deposit), lambda: deposit_out
    )
    return flow_out, arrived.T, deposit_out


def solution(mesh):
    each = ("passage", "span")
    tile = P(None, "passage", "span")
    rows = P(each, None)
    return jax.shard_map(
        local,
        mesh=mesh,
        in_specs=(tile, P("passage", "span"), rows, rows, P(each), P(each), rows),
        out_specs=(tile, rows, rows),
        check_vma=False,
    )
```

```python
import functools

import jax
import jax.numpy as jnp
from jax import lax
from jax.experimental import pallas as pl
from jax.experimental.pallas import tpu as pltpu
from jax.sharding import PartitionSpec as P

FLOW_STEP = 0.1
COND_STEP = 0.2
MOVE_STEP = 0.5
DEVICES = 128
COUNT = 8192
WIDTH = 32
CAP = 72
HALF = 36
ROWS = 20
LIST = 119
CHUNK = 1024
BLOCK = 256
NT = (((1,), (1,)), ((), ()))
F32 = jnp.float32
BF16 = jnp.bfloat16
F8 = jnp.float8_e5m2
LIFT = 2.0**20
I32 = jnp.int32


def iota(shape, dim):
    return lax.broadcasted_iota(I32, shape, dim)


def hot(index, size):
    return (iota((size, index.shape[1]), 0) == index).astype(F32)


def split(x):
    high = x.astype(BF16)
    return high, (x - high.astype(F32)).astype(BF16)


def spread(row, size):
    return jnp.broadcast_to(row, (size, row.shape[1]))


def counting(size, lanes):
    return iota((size, lanes), 0).astype(F32).astype(BF16)


def ones_at(row, size):
    here = counting(size, row.shape[1]) == jnp.broadcast_to(row.astype(BF16), (size, row.shape[1]))
    return jnp.where(here, jnp.ones(here.shape, BF16), jnp.zeros(here.shape, BF16))


def send_kernel(
    vel_h, visc_h, rec_h, own_h, cell_h, wall_h, out, aux, top, bottom, left, right,
    vel, rec, own, cell, wall, table, val, meta, a_ref, b_ref, a_low, b_low, a2_ref, b2_ref, acc, acc_low, acc2, base, mix, sems,
):
    copies = [
        pltpu.make_async_copy(source, target, sems.at[i])
        for i, (source, target) in enumerate(
            ((vel_h, vel.at[0:3]), (visc_h, vel.at[3]), (own_h, own), (cell_h, cell), (wall_h, wall), (rec_h, rec))
        )
    ]
    for copy in copies:
        copy.start()
    acc[...] = jnp.zeros_like(acc)
    acc_low[...] = jnp.zeros_like(acc_low)
    acc2[...] = jnp.zeros_like(acc2)
    base[...] = jnp.zeros_like(base)
    earlier = (iota((BLOCK, BLOCK), 0) < iota((BLOCK, BLOCK), 1)).astype(F32).astype(BF16)
    for copy in copies[:2]:
        copy.wait()
    for c in range(4):
        turned = vel[c].T
        left[2 * c : 2 * c + 2, :] = turned[0:2]
        right[2 * c : 2 * c + 2, :] = turned[254:256]
        top[2 * c : 2 * c + 2, :] = vel[c, 0:2, :]
        bottom[2 * c : 2 * c + 2, :] = vel[c, 126:128, :]
        if c < 3:
            high, low = split(turned)
            table[pl.ds(c * 256, 256), 0:128] = high
            table[pl.ds(c * 256, 256), 128:256] = low
    for copy in copies[2:]:
        copy.wait()

    def prepare(i):
        if True:
            lanes = pl.ds(pl.multiple_of(i * BLOCK, BLOCK), BLOCK)
            owner = own[0:1, lanes]
            place = cell[0:1, lanes]
            slot = wall[0:1, lanes]
            wall_dev = (owner >> 3) * 8 + (slot >> 16)
            both = jnp.concatenate([ones_at(owner.astype(F32), 128), ones_at(wall_dev.astype(F32), 128)], axis=0)
            before = jnp.dot(both, earlier, preferred_element_type=F32)
            both = both.astype(F32)
            start = base[...]
            picked = both * (before + jnp.concatenate([start, start], axis=1))
            rank = jnp.sum(picked[:128], axis=0, keepdims=True)
            rank2 = jnp.sum(picked[128:], axis=0, keepdims=True)
            base[...] = start + jnp.sum(both, axis=1, keepdims=True)

            row_hot = ones_at((place >> 8).astype(F32), 128)
            looked = jnp.dot(table[...], jnp.concatenate([row_hot, row_hot], axis=0), preferred_element_type=F32)
            col_is = iota((256, BLOCK), 0) == (place & 255)
            fluid = jnp.concatenate(
                [
                    jnp.sum(jnp.where(col_is, looked[c * 256 : (c + 1) * 256], 0.0), axis=0, keepdims=True)
                    for c in range(3)
                ],
                axis=0,
            )
            r = rec[:, lanes]
            old = r[0:3]
            new = old + jax.nn.sigmoid(r[3:4]) * (fluid - old)
            values = jnp.concatenate([new, r[3:6], r[6:9] + MOVE_STEP * new, r[9:]], axis=0)
            energy = jnp.sum(new * new, axis=0, keepdims=True)
            mass = r[5:6]
            soft = jnp.maximum(mass, 0.0) + jnp.log1p(jnp.exp(-jnp.abs(mass)))
            amount = jax.nn.sigmoid(r[4:5]) * soft * energy / (1.0 + energy)
            first = ((slot >> 8) & 3) * 64 + ((slot >> 10) & 63)
            second = slot & 255
            aux[0:1, lanes] = amount
            aux[1:2, lanes] = (first * 256 + second).astype(F32)
            aux[2:3, lanes] = wall_dev.astype(F32)
            aux[3:4, lanes] = rank2

            highs = values.astype(BF16).astype(F32)
            val[0:32, lanes] = highs
            val[32:64, lanes] = (values - highs) * LIFT
            late = rank >= HALF
            late2 = rank2 >= 64.0
            high = amount.astype(BF16).astype(F32)
            meta[0:1, lanes] = jnp.where(late, rank - HALF, rank)
            meta[1:2, lanes] = owner.astype(F32) + jnp.where(late, 128.0, 0.0)
            meta[2:3, lanes] = jnp.where(rank2 < LIST, jnp.where(late2, rank2 - 64.0, rank2), 64.0)
            meta[3:4, lanes] = wall_dev.astype(F32) + jnp.where(late2, 128.0, 0.0)
            meta[4:5, lanes] = first.astype(F32)
            meta[5:6, lanes] = second.astype(F32)
            meta[6:7, lanes] = high
            meta[7:8, lanes] = amount - high

    def place_hot(t):
        lanes = pl.ds(pl.multiple_of(t * CHUNK, CHUNK), CHUNK)
        hot_owner = ones_at(meta[1:2, lanes], 256)
        b_ref[...] = hot_owner
        b_low[...] = hot_owner.astype(F8)

    def place_part(t, part, target):
        lanes = pl.ds(pl.multiple_of(t * CHUNK, CHUNK), CHUNK)
        row = lambda ref, i, size: jnp.broadcast_to(ref[i : i + 1, lanes].astype(BF16), (size, CHUNK))
        step = row(meta, 0, 32)
        zero = jnp.zeros((32, CHUNK), BF16)
        main = counting(32, CHUNK) == step
        for f in range(WIDTH):
            to = (f % 8 * 4 + f // 8) * 32
            target[pl.ds(to, 32), :] = jnp.where(main, row(val, part * 32 + f, 32), zero).astype(target.dtype)
        whole = val[part * 32 : part * 32 + 32, lanes].astype(BF16)
        for e in range(4):
            target[pl.ds(1024 + e * 32, 32), :] = jnp.where(step == 32 + e, whole, zero).astype(target.dtype)

    def place_wall(t):
        lanes = pl.ds(pl.multiple_of(t * CHUNK, CHUNK), CHUNK)
        row = lambda ref, i, size: jnp.broadcast_to(ref[i : i + 1, lanes].astype(BF16), (size, CHUNK))
        main = counting(64, CHUNK) == row(meta, 2, 64)
        zero = jnp.zeros((64, CHUNK), BF16)
        b2_ref[...] = ones_at(meta[3:4, lanes], 256)
        for v in range(4):
            a2_ref[pl.ds(v * 64, 64), :] = jnp.where(main, row(meta, 4 + v, 64), zero)

    pieces = CHUNK // BLOCK

    def add(total, left_ref, right_ref):
        total[...] += lax.dot_general(left_ref[...], right_ref[...], NT, preferred_element_type=F32)

    def first_blocks(i, carry):
        prepare(i)
        return carry

    lax.fori_loop(0, pieces, first_blocks, 0)

    def chunk(t, ahead):
        place_hot(t)
        place_part(t, 0, a_ref)
        place_part(t, 1, a_low)
        place_wall(t)
        add(acc, a_ref, b_ref)
        if ahead:
            prepare((t + 1) * pieces)
        add(acc_low, a_low, b_low)
        if ahead:
            prepare((t + 1) * pieces + 1)
        add(acc2, a2_ref, b2_ref)
        if ahead:
            for piece in range(2, pieces):
                prepare((t + 1) * pieces + piece)

    def with_next(t, carry):
        chunk(t, True)
        return carry

    lax.fori_loop(0, COUNT // CHUNK - 1, with_next, 0)
    chunk(COUNT // CHUNK - 1, False)

    def summed(c):
        low = pl.multiple_of(c * 128, 128)
        return acc[pl.ds(low, 128), :] + acc_low[pl.ds(low, 128), :] * (1.0 / LIFT)

    def main_rows(c, carry):
        both = summed(c)
        for h in range(2):
            out[pl.ds(h * 8 + c, 128, stride=ROWS), :] = both[:, h * 128 : (h + 1) * 128].T
        return carry

    lax.fori_loop(0, 8, main_rows, 0)
    rest = summed(8)
    for h in range(2):
        mix[h] = rest[:, h * 128 : (h + 1) * 128]
    for f in range(WIDTH):
        to = 4 * (f // 8 * 8 + 7 - f % 8)
        for h in range(2):
            mix[2 + h, to : to + 4, :] = mix[h, pl.ds(f, 4, stride=32), :]
    for h in range(2):
        out[pl.ds(16 + h, 128, stride=ROWS), :] = mix[2 + h].T
    spot = acc2[0:64, :] * 256.0 + acc2[64:128, :]
    amount = acc2[128:192, :] + acc2[192:256, :]
    spot = jnp.concatenate([spot[:, :128], spot[:, 128:]], axis=0).T
    amount = jnp.concatenate([amount[:, :128], amount[:, 128:]], axis=0).T
    most = jnp.max(base[128:, :])
    lane = iota((128, 128), 1)

    def with_corners(x, row):
        for side in range(2):
            for c in range(4):
                cell_of = vel[c, row : row + 1, 255 * side : 255 * side + 1]
                x = jnp.where(lane == LIST + 4 * side + c, cell_of, x)
        return x

    out[pl.ds(18, 128, stride=ROWS), :] = jnp.where(lane == 127, most, with_corners(spot, 0))
    out[pl.ds(19, 128, stride=ROWS), :] = with_corners(amount, 127)


def send(velocity, viscosity, records_t, owner, cell, wall_slot):
    return pl.pallas_call(
        send_kernel,
        out_shape=(
            jax.ShapeDtypeStruct((DEVICES * ROWS, 128), F32),
            jax.ShapeDtypeStruct((4, COUNT), F32),
            jax.ShapeDtypeStruct((8, 256), F32),
            jax.ShapeDtypeStruct((8, 256), F32),
            jax.ShapeDtypeStruct((8, 128), F32),
            jax.ShapeDtypeStruct((8, 128), F32),
        ),
        in_specs=[pl.BlockSpec(memory_space=pl.ANY)] * 6,
        out_specs=[pl.BlockSpec(memory_space=pltpu.VMEM)] * 6,
        scratch_shapes=[
            pltpu.VMEM((4, 128, 256), F32),
            pltpu.VMEM((WIDTH, COUNT), F32),
            pltpu.VMEM((1, COUNT), I32),
            pltpu.VMEM((1, COUNT), I32),
            pltpu.VMEM((1, COUNT), I32),
            pltpu.VMEM((768, 256), BF16),
            pltpu.VMEM((64, COUNT), F32),
            pltpu.VMEM((8, COUNT), F32),
            pltpu.VMEM((1152, CHUNK), BF16),
            pltpu.VMEM((256, CHUNK), BF16),
            pltpu.VMEM((1152, CHUNK), F8),
            pltpu.VMEM((256, CHUNK), F8),
            pltpu.VMEM((256, CHUNK), BF16),
            pltpu.VMEM((256, CHUNK), BF16),
            pltpu.VMEM((1152, 256), F32),
            pltpu.VMEM((1152, 256), F32),
            pltpu.VMEM((256, 256), F32),
            pltpu.VMEM((256, 128), F32),
            pltpu.VMEM((4, 128, 128), F32),
            pltpu.SemaphoreType.DMA((6,)),
        ],
        compiler_params=pltpu.CompilerParams(vmem_limit_bytes=56 << 20),
        name="send",
    )(velocity, viscosity, records_t, owner, cell, wall_slot)


def conduct(t):
    rows = iota(t.shape, 0)
    cols = iota(t.shape, 1)
    for repeat in range(2):
        up = jnp.where(rows == 0, t, pltpu.roll(t, 1, 0))
        down = jnp.where(rows == t.shape[0] - 1, t, pltpu.roll(t, t.shape[0] - 1, 0))
        left = jnp.where(cols == 0, t, pltpu.roll(t, 1, 1))
        right = jnp.where(cols == t.shape[1] - 1, t, pltpu.roll(t, t.shape[1] - 1, 1))
        t = t + COND_STEP * ((down + up + right + left) - 4.0 * t)
    return t


def flow(where, got, vel, visc, north, south, west, east, flow_out, field):
    pi, si = where[0], where[1]
    row, col = iota((136, 384), 0), iota((136, 384), 1)
    outside = (
        ((pi == 0) & (row >= 132))
        | ((pi == 15) & (row >= 128) & (row < 132))
        | ((si == 0) & (col >= 320))
        | ((si == 7) & (col >= 256) & (col < 320))
    )
    side_row, side_col = iota((8, 128), 0), iota((8, 128), 1)
    west_cells, east_cells = west[...].T, east[...].T
    for c in range(4):
        field[c, :, 256:384] = jnp.zeros((136, 128), F32)
        field[c, 128:136, 0:256] = jnp.zeros((8, 256), F32)
        field[c, 0:128, 0:256] = vel[c] if c < 3 else visc[...]
        field[c, 134:136, 0:256] = north[2 * c : 2 * c + 2, :]
        field[c, 128:130, 0:256] = south[2 * c : 2 * c + 2, :]
        field[c, 0:128, 382:384] = west_cells[:, 2 * c : 2 * c + 2]
        field[c, 0:128, 256:258] = east_cells[:, 2 * c : 2 * c + 2]
    corners = [jnp.zeros((8, 128), F32)] * 4
    for down in range(2):
        for over in range(2):
            there_p = pi + 2 * down - 1
            there_s = si + 2 * over - 1
            inside = (there_p >= 0) & (there_p < 16) & (there_s >= 0) & (there_s < 8)
            source = jnp.where(inside, there_p * 8 + there_s, 0)
            cells = got[pl.ds(source * ROWS + 19 - down, 1), :]
            cells = jnp.broadcast_to(jnp.where(inside, cells, 0.0), (8, 128))
            to_row, to_col = 7 * (1 - down), 127 * (1 - over)
            here = (side_row == to_row) & (side_col == to_col)
            for c in range(4):
                turn = (to_col - (LIST + 4 * (1 - over) + c)) % 128
                corners[c] = jnp.where(here, pltpu.roll(cells, turn, 1), corners[c])
    for c in range(4):
        field[c, 128:136, 256:384] = corners[c]
    nu = field[3]
    faces = []
    for axis, size in ((1, 384), (0, 136)):
        for shift in (size - 1, 1):
            faces.append((0.5 * (pltpu.roll(nu, shift, axis) + nu), shift, axis))
    for c in range(3):
        f = field[c]
        for sweep in range(2):
            flux = jnp.zeros_like(f)
            for face, shift, axis in faces:
                flux = flux + face * (pltpu.roll(f, shift, axis) - f)
            f = f + FLOW_STEP * flux
            if sweep == 0:
                f = jnp.where(outside, 0.0, f)
        flow_out[c] = f[0:128, 0:256]


def receive_kernel(
    where, got, deposit, vel, visc, north, south, west, east,
    arrived, deposit_out, flow_out, total, most, h1_ref, h2_ref, h1_low, h2_low, acc, acc_low, field,
):
    flow(where, got, vel, visc, north, south, west, east, flow_out, field)
    lane = iota((8, 128), 1)
    wide = iota((64, 128), 1)
    even = ((wide >= 32) & (wide < 36)) | ((wide >= 96) & (wide < 100))
    odd = ((wide >= 64) & (wide < 68)) | (wide < 4)
    upto = iota((256, 128), 0).astype(F32).astype(BF16)

    groups = DEVICES // 16

    def stack(row):
        return jnp.concatenate([got[pl.ds(row + g * (16 * ROWS), 8), :] for g in range(groups)], axis=0)

    def fan(row):
        one = [got[pl.ds(row + g * (16 * ROWS), 1), :] for g in range(groups)]
        return jnp.concatenate(
            [pltpu.roll(jnp.broadcast_to(x, (8, 128)), 4, 1, stride=4, stride_axis=0) for x in one], axis=0
        )

    def unpack(s, carry):
        at = s * CAP
        tile, off = at >> 7, at & 127
        halves = []
        for h in range(2):
            body = stack(s * ROWS + 8 * h)
            rest = fan(s * ROWS + 16 + h)
            halves.append((jnp.where(even, rest, body), jnp.where(odd, rest, body)))
        for k in range(4):
            last = pltpu.roll(halves[1][k % 2], HALF, 1)
            piece = jnp.where((wide >= 32 * k) & (wide < 32 * k + HALF) | (wide < 32 * k + HALF - 128), halves[0][k % 2], last)
            piece = pltpu.roll(piece, (at - 32 * k) & 127, 1)
            over = off + CAP > 128
            for g in range(groups):
                mine = piece[8 * g : 8 * g + 8]
                to = pl.ds(pl.multiple_of((g * 9 + tile) * 128, 128), 128)
                made = jnp.where(lane >= off, mine, arrived[8 * k : 8 * k + 8, to])
                arrived[8 * k : 8 * k + 8, to] = made
                to = pl.ds(pl.multiple_of((g * 9 + tile + over.astype(I32)) * 128, 128), 128)
                arrived[8 * k : 8 * k + 8, to] = jnp.where(over, mine, made)
        return carry

    def build(g, slot):
        spot16 = got[pl.ds(g * (16 * ROWS) + 18, 16, stride=ROWS), :].astype(I32)
        amount16 = got[pl.ds(g * (16 * ROWS) + 19, 16, stride=ROWS), :]
        amount16 = jnp.where(iota((16, 128), 1) < LIST, amount16, 0.0)
        firsts = (spot16 >> 8).astype(F32)
        seconds = (spot16 & 255).astype(F32)
        highs = amount16.astype(BF16).astype(F32)
        lows = (amount16 - highs) * LIFT
        one = jnp.ones((256, 128), BF16)
        zero = jnp.zeros((256, 128), BF16)
        for s in range(16):
            here = pl.ds(s * 128, 128)
            row = lambda x: jnp.broadcast_to(x[s : s + 1].astype(BF16), (256, 128))
            first = jnp.where(upto == row(firsts), one, zero)
            h1_ref[slot, :, here] = first
            h1_low[slot, :, here] = first.astype(F8)
            same = upto == row(seconds)
            h2_ref[slot, :, here] = jnp.where(same, row(highs), zero)
            h2_low[slot, :, here] = jnp.where(same, row(lows), zero).astype(F8)

    def add(slot):
        acc[...] += lax.dot_general(h1_ref[slot], h2_ref[slot], NT, preferred_element_type=F32)
        acc_low[...] += lax.dot_general(h1_low[slot], h2_low[slot], NT, preferred_element_type=F32)

    acc[...] = jnp.zeros_like(acc)
    acc_low[...] = jnp.zeros_like(acc_low)
    build(0, 0)

    def pair_of_groups(u, carry):
        unpack(4 * u, 0)
        build(2 * u + 1, 1)
        unpack(4 * u + 1, 0)
        add(0)
        unpack(4 * u + 2, 0)
        build(jnp.minimum(2 * u + 2, 7), 0)
        unpack(4 * u + 3, 0)
        add(1)
        return carry

    lax.fori_loop(0, 4, pair_of_groups, 0)
    struck = acc[...] + acc_low[...] * (1.0 / LIFT)
    struck = jnp.concatenate([struck[64 * c : 64 * c + 64] for c in range(4)], axis=1)
    total[...] = struck
    had = deposit[...]
    deposit_out[...] = conduct(had + jnp.exp(-had) * struck)
    counts = got[pl.ds(18, DEVICES, stride=ROWS), :]
    most[...] = jnp.max(counts[:, 127:], axis=0, keepdims=True).reshape(1, 1)


def receive(where, got, deposit, velocity, viscosity, halos):
    return pl.pallas_call(
        receive_kernel,
        out_shape=(
            jax.ShapeDtypeStruct((WIDTH, DEVICES * CAP), F32),
            jax.ShapeDtypeStruct((64, 1024), F32),
            jax.ShapeDtypeStruct((3, 128, 256), F32),
            jax.ShapeDtypeStruct((64, 1024), F32),
            jax.ShapeDtypeStruct((1, 1), F32),
        ),
        in_specs=[pl.BlockSpec(memory_space=pltpu.SMEM)] + [pl.BlockSpec(memory_space=pltpu.VMEM)] * 8,
        out_specs=[pl.BlockSpec(memory_space=pltpu.VMEM)] * 5,
        scratch_shapes=[
            pltpu.VMEM((2, 256, 2048), BF16),
            pltpu.VMEM((2, 256, 2048), BF16),
            pltpu.VMEM((2, 256, 2048), F8),
            pltpu.VMEM((2, 256, 2048), F8),
            pltpu.VMEM((256, 256), F32),
            pltpu.VMEM((256, 256), F32),
            pltpu.VMEM((4, 136, 384), F32),
        ],
        compiler_params=pltpu.CompilerParams(vmem_limit_bytes=48 << 20),
        name="receive",
    )(where, got, deposit, velocity, viscosity, *halos)


def shifted(cells, axis, up):
    count = lax.axis_size(axis)
    pairs = [(i, i + 1) if up else (i + 1, i) for i in range(count - 1)]
    return lax.ppermute(cells, axis, pairs)


def conduct_plain(thickness):
    for repeat in range(2):
        padded = jnp.pad(thickness, 1, mode="edge")
        beside = padded[2:, 1:-1] + padded[:-2, 1:-1] + padded[1:-1, 2:] + padded[1:-1, :-2]
        thickness = thickness + COND_STEP * (beside - 4.0 * thickness)
    return thickness


def rest_of_lists(total, most, aux, deposit):
    amount, spot = aux[0], aux[1]
    wall_dev, rank = aux[2].astype(I32), aux[3].astype(I32)

    def one_round(state):
        turn, total = state
        low = turn * LIST
        taken = (rank >= low) & (rank < low + LIST)
        index = jnp.where(taken, wall_dev * 128 + rank - low, DEVICES * 128)
        lists = jnp.zeros((DEVICES * 128, 2), F32)
        lists = lists.at[index].set(jnp.stack([amount, spot], axis=1), mode="drop")
        lists = lists.reshape(DEVICES, 128, 2).transpose(0, 2, 1).reshape(DEVICES, 1, 256)
        lists = lax.all_to_all(lists, ("passage", "span"), 0, 0, tiled=True).reshape(DEVICES, 2, 128)
        code = lists[:, 1].reshape(-1).astype(I32)
        first, second = code >> 8, code & 255
        place = (first & 63) * 1024 + (first >> 6) * 256 + second
        added = jnp.zeros((64 * 1024,), F32).at[place].add(lists[:, 0].reshape(-1))
        return turn + 1, total + added.reshape(64, 1024)

    total = lax.while_loop(lambda state: state[0] * LIST < most.astype(I32), one_round, (1, total))[1]
    return conduct_plain(deposit + jnp.exp(-deposit) * total)


def local(velocity, viscosity, records, owner, cell, wall_slot, deposit):
    packed, aux, top, bottom, left, right = send(
        velocity, viscosity, records.T, owner.reshape(1, COUNT), cell.reshape(1, COUNT), wall_slot.reshape(1, COUNT)
    )
    got = lax.all_to_all(packed.reshape(DEVICES, 1, ROWS * 128), ("passage", "span"), 0, 0, tiled=True)
    halos = (
        shifted(bottom, "passage", True),
        shifted(top, "passage", False),
        shifted(right, "span", True),
        shifted(left, "span", False),
    )
    where = jnp.stack([lax.axis_index("passage"), lax.axis_index("span")]).astype(I32)
    arrived, deposit_out, flow_out, total, most = receive(
        where, got.reshape(DEVICES * ROWS, 128), deposit, velocity, viscosity, halos
    )
    most = most[0, 0]
    deposit_out = lax.cond(
        most > LIST, lambda: rest_of_lists(total, most, aux, deposit), lambda: deposit_out
    )
    return flow_out, arrived.T, deposit_out


def solution(mesh):
    each = ("passage", "span")
    tile = P(None, "passage", "span")
    rows = P(each, None)
    return jax.shard_map(
        local,
        mesh=mesh,
        in_specs=(tile, P("passage", "span"), rows, rows, P(each), P(each), rows),
        out_specs=(tile, rows, rows),
        check_vma=False,
    )
```

```python
import functools

import jax
import jax.numpy as jnp
from jax import lax
from jax.experimental import pallas as pl
from jax.experimental.pallas import tpu as pltpu
from jax.sharding import PartitionSpec as P

FLOW_STEP = 0.1
COND_STEP = 0.2
MOVE_STEP = 0.5
DEVICES = 128
COUNT = 8192
WIDTH = 32
CAP = 72
HALF = 36
ROWS = 20
LIST = 119
CHUNK = 1024
BLOCK = 256
NT = (((1,), (1,)), ((), ()))
F32 = jnp.float32
BF16 = jnp.bfloat16
F8 = jnp.float8_e5m2
LIFT = 2.0**20
I32 = jnp.int32


def iota(shape, dim):
    return lax.broadcasted_iota(I32, shape, dim)


def hot(index, size):
    return (iota((size, index.shape[1]), 0) == index).astype(F32)


def split(x):
    high = x.astype(BF16)
    return high, (x - high.astype(F32)).astype(BF16)


def spread(row, size):
    return jnp.broadcast_to(row, (size, row.shape[1]))


def counting(size, lanes):
    return iota((size, lanes), 0).astype(F32).astype(BF16)


def ones_at(row, size):
    here = counting(size, row.shape[1]) == jnp.broadcast_to(row.astype(BF16), (size, row.shape[1]))
    return jnp.where(here, jnp.ones(here.shape, BF16), jnp.zeros(here.shape, BF16))


def send_kernel(
    vel_h, visc_h, rec_h, own_h, cell_h, wall_h, out, aux, top, bottom, left, right,
    vel, rec, own, cell, wall, table, table_low, val, meta, a_ref, b_ref, a_low, b_low, a2_ref, b2_ref, acc, acc_low, acc2, base, mix, sems,
):
    copies = [
        pltpu.make_async_copy(source, target, sems.at[i])
        for i, (source, target) in enumerate(
            ((own_h, own), (wall_h, wall), (cell_h, cell), (vel_h, vel.at[0:3]), (visc_h, vel.at[3]), (rec_h, rec))
        )
    ]
    for copy in copies:
        copy.start()
    acc[...] = jnp.zeros_like(acc)
    acc_low[...] = jnp.zeros_like(acc_low)
    acc2[...] = jnp.zeros_like(acc2)
    base[...] = jnp.zeros_like(base)
    earlier = (iota((BLOCK, BLOCK), 0) < iota((BLOCK, BLOCK), 1)).astype(F32).astype(BF16)

    def rank_chunk(t):
        every = []
        for b in range(CHUNK // BLOCK):
            lanes = pl.ds(pl.multiple_of(t * CHUNK + b * BLOCK, BLOCK), BLOCK)
            owner = own[0:1, lanes]
            wall_dev = (owner >> 3) * 8 + (wall[0:1, lanes] >> 16)
            every += [ones_at(owner.astype(F32), 128), ones_at(wall_dev.astype(F32), 128)]
        every = jnp.concatenate(every, axis=0)
        before = jnp.dot(every, earlier, preferred_element_type=F32)
        start = base[...]
        for b in range(CHUNK // BLOCK):
            lanes = pl.ds(pl.multiple_of(t * CHUNK + b * BLOCK, BLOCK), BLOCK)
            both = every[b * 256 : b * 256 + 256].astype(F32)
            picked = both * (before[b * 256 : b * 256 + 256] + jnp.concatenate([start, start], axis=1))
            meta[8:9, lanes] = jnp.sum(picked[:128], axis=0, keepdims=True)
            meta[9:10, lanes] = jnp.sum(picked[128:], axis=0, keepdims=True)
            start = start + jnp.sum(both, axis=1, keepdims=True)
        base[...] = start

    def prepare(i):
        if 1:
            lanes = pl.ds(pl.multiple_of(i * BLOCK, BLOCK), BLOCK)
            owner = own[0:1, lanes]
            place = cell[0:1, lanes]
            slot = wall[0:1, lanes]
            wall_dev = (owner >> 3) * 8 + (slot >> 16)
            rank = meta[8:9, lanes]
            rank2 = meta[9:10, lanes]
            row_hot = ones_at(((place & 128) + (place >> 8)).astype(F32), 256)
            looked = jnp.dot(table[...], row_hot, preferred_element_type=F32)
            looked_low = jnp.dot(table_low[...], row_hot.astype(F8), preferred_element_type=F32)
            col_is = iota((128, BLOCK), 0) == (place & 127)
            fluid = jnp.concatenate(
                [
                    jnp.sum(
                        jnp.where(
                            col_is,
                            looked[c * 128 : c * 128 + 128] + looked_low[c * 128 : c * 128 + 128] * (1.0 / LIFT),
                            0.0,
                        ),
                        axis=0,
                        keepdims=True,
                    )
                    for c in range(3)
                ],
                axis=0,
            )
            r = rec[:, lanes]
            old = r[0:3]
            new = old + jax.nn.sigmoid(r[3:4]) * (fluid - old)
            values = jnp.concatenate([new, r[3:6], r[6:9] + MOVE_STEP * new, r[9:]], axis=0)
            energy = jnp.sum(new * new, axis=0, keepdims=True)
            mass = r[5:6]
            soft = jnp.maximum(mass, 0.0) + jnp.log1p(jnp.exp(-jnp.abs(mass)))
            amount = jax.nn.sigmoid(r[4:5]) * soft * energy / (1.0 + energy)
            first = ((slot >> 8) & 3) * 64 + ((slot >> 10) & 63)
            second = slot & 255
            aux[0:1, lanes] = amount
            aux[1:2, lanes] = (first * 256 + second).astype(F32)
            aux[2:3, lanes] = wall_dev.astype(F32)
            aux[3:4, lanes] = rank2

            highs = values.astype(BF16).astype(F32)
            val[0:32, lanes] = highs
            val[32:64, lanes] = (values - highs) * LIFT
            late = rank >= HALF
            late2 = rank2 >= 64.0
            high = amount.astype(BF16).astype(F32)
            meta[0:1, lanes] = jnp.where(late, rank - HALF, rank)
            meta[1:2, lanes] = owner.astype(F32) + jnp.where(late, 128.0, 0.0)
            meta[2:3, lanes] = jnp.where(rank2 < LIST, jnp.where(late2, rank2 - 64.0, rank2), 64.0)
            meta[3:4, lanes] = wall_dev.astype(F32) + jnp.where(late2, 128.0, 0.0)
            meta[4:5, lanes] = first.astype(F32)
            meta[5:6, lanes] = second.astype(F32)
            meta[6:7, lanes] = high
            meta[7:8, lanes] = amount - high

    def place_hot(t):
        lanes = pl.ds(pl.multiple_of(t * CHUNK, CHUNK), CHUNK)
        hot_owner = ones_at(meta[1:2, lanes], 256)
        b_ref[...] = hot_owner
        b_low[...] = hot_owner.astype(F8)

    def place_part(t, part, target):
        lanes = pl.ds(pl.multiple_of(t * CHUNK, CHUNK), CHUNK)
        row = lambda ref, i, size: jnp.broadcast_to(ref[i : i + 1, lanes].astype(BF16), (size, CHUNK))
        step = row(meta, 0, 32)
        zero = jnp.zeros((32, CHUNK), BF16)
        main = counting(32, CHUNK) == step
        for f in range(WIDTH):
            to = (f % 8 * 4 + f // 8) * 32
            target[pl.ds(to, 32), :] = jnp.where(main, row(val, part * 32 + f, 32), zero).astype(target.dtype)
        whole = val[part * 32 : part * 32 + 32, lanes].astype(BF16)
        for e in range(4):
            target[pl.ds(1024 + e * 32, 32), :] = jnp.where(step == 32 + e, whole, zero).astype(target.dtype)

    def place_wall(t):
        lanes = pl.ds(pl.multiple_of(t * CHUNK, CHUNK), CHUNK)
        row = lambda ref, i, size: jnp.broadcast_to(ref[i : i + 1, lanes].astype(BF16), (size, CHUNK))
        main = counting(64, CHUNK) == row(meta, 2, 64)
        zero = jnp.zeros((64, CHUNK), BF16)
        b2_ref[...] = ones_at(meta[3:4, lanes], 256)
        for v in range(4):
            a2_ref[pl.ds(v * 64, 64), :] = jnp.where(main, row(meta, 4 + v, 64), zero)

    pieces = CHUNK // BLOCK

    def add(total, left_ref, right_ref):
        total[...] += lax.dot_general(left_ref[...], right_ref[...], NT, preferred_element_type=F32)

    def first_blocks(i, carry):
        prepare(i)
        return carry

    for copy in copies[:3]:
        copy.wait()
    rank_chunk(0)
    for copy in copies[3:5]:
        copy.wait()
    for c in range(4):
        turned = vel[c].T
        left[2 * c : 2 * c + 2, :] = turned[0:2]
        right[2 * c : 2 * c + 2, :] = turned[254:256]
        top[2 * c : 2 * c + 2, :] = vel[c, 0:2, :]
        bottom[2 * c : 2 * c + 2, :] = vel[c, 126:128, :]
        if c < 3:
            high = turned.astype(BF16)
            low = ((turned - high.astype(F32)) * LIFT).astype(F8)
            for half in range(2):
                table[pl.ds(c * 128, 128), half * 128 : half * 128 + 128] = high[half * 128 : half * 128 + 128]
                table_low[pl.ds(c * 128, 128), half * 128 : half * 128 + 128] = low[half * 128 : half * 128 + 128]
    copies[5].wait()
    lax.fori_loop(0, pieces, first_blocks, 0)

    def chunk(t, ahead):
        place_hot(t)
        place_part(t, 0, a_ref)
        place_part(t, 1, a_low)
        place_wall(t)
        add(acc, a_ref, b_ref)
        if ahead:
            rank_chunk(t + 1)
            prepare((t + 1) * pieces)
        add(acc_low, a_low, b_low)
        if ahead:
            prepare((t + 1) * pieces + 1)
        add(acc2, a2_ref, b2_ref)
        if ahead:
            for piece in range(2, pieces):
                prepare((t + 1) * pieces + piece)

    def with_next(t, carry):
        chunk(t, True)
        return carry

    lax.fori_loop(0, COUNT // CHUNK - 1, with_next, 0)
    chunk(COUNT // CHUNK - 1, False)

    def summed(c):
        low = pl.multiple_of(c * 128, 128)
        return acc[pl.ds(low, 128), :] + acc_low[pl.ds(low, 128), :] * (1.0 / LIFT)

    def main_rows(c, carry):
        both = summed(c)
        for h in range(2):
            out[pl.ds(h * 8 + c, 128, stride=ROWS), :] = both[:, h * 128 : (h + 1) * 128].T
        return carry

    lax.fori_loop(0, 8, main_rows, 0)
    rest = summed(8)
    for h in range(2):
        mix[h] = rest[:, h * 128 : (h + 1) * 128]
    for f in range(WIDTH):
        to = 4 * (f // 8 * 8 + 7 - f % 8)
        for h in range(2):
            mix[2 + h, to : to + 4, :] = mix[h, pl.ds(f, 4, stride=32), :]
    for h in range(2):
        out[pl.ds(16 + h, 128, stride=ROWS), :] = mix[2 + h].T
    spot = acc2[0:64, :] * 256.0 + acc2[64:128, :]
    amount = acc2[128:192, :] + acc2[192:256, :]
    spot = jnp.concatenate([spot[:, :128], spot[:, 128:]], axis=0).T
    amount = jnp.concatenate([amount[:, :128], amount[:, 128:]], axis=0).T
    most = jnp.max(base[128:, :])
    lane = iota((128, 128), 1)

    def with_corners(x, row):
        for side in range(2):
            for c in range(4):
                cell_of = vel[c, row : row + 1, 255 * side : 255 * side + 1]
                x = jnp.where(lane == LIST + 4 * side + c, cell_of, x)
        return x

    out[pl.ds(18, 128, stride=ROWS), :] = jnp.where(lane == 127, most, with_corners(spot, 0))
    out[pl.ds(19, 128, stride=ROWS), :] = with_corners(amount, 127)


def send(velocity, viscosity, records_t, owner, cell, wall_slot):
    return pl.pallas_call(
        send_kernel,
        out_shape=(
            jax.ShapeDtypeStruct((DEVICES * ROWS, 128), F32),
            jax.ShapeDtypeStruct((4, COUNT), F32),
            jax.ShapeDtypeStruct((8, 256), F32),
            jax.ShapeDtypeStruct((8, 256), F32),
            jax.ShapeDtypeStruct((8, 128), F32),
            jax.ShapeDtypeStruct((8, 128), F32),
        ),
        in_specs=[pl.BlockSpec(memory_space=pl.ANY)] * 6,
        out_specs=[pl.BlockSpec(memory_space=pltpu.VMEM)] * 6,
        scratch_shapes=[
            pltpu.VMEM((4, 128, 256), F32),
            pltpu.VMEM((WIDTH, COUNT), F32),
            pltpu.VMEM((1, COUNT), I32),
            pltpu.VMEM((1, COUNT), I32),
            pltpu.VMEM((1, COUNT), I32),
            pltpu.VMEM((384, 256), BF16),
            pltpu.VMEM((384, 256), F8),
            pltpu.VMEM((64, COUNT), F32),
            pltpu.VMEM((16, COUNT), F32),
            pltpu.VMEM((1152, CHUNK), BF16),
            pltpu.VMEM((256, CHUNK), BF16),
            pltpu.VMEM((1152, CHUNK), F8),
            pltpu.VMEM((256, CHUNK), F8),
            pltpu.VMEM((256, CHUNK), BF16),
            pltpu.VMEM((256, CHUNK), BF16),
            pltpu.VMEM((1152, 256), F32),
            pltpu.VMEM((1152, 256), F32),
            pltpu.VMEM((256, 256), F32),
            pltpu.VMEM((256, 128), F32),
            pltpu.VMEM((4, 128, 128), F32),
            pltpu.SemaphoreType.DMA((6,)),
        ],
        compiler_params=pltpu.CompilerParams(vmem_limit_bytes=48 << 20),
        name="send",
    )(*(pltpu.with_memory_space_constraint(x, pltpu.HBM) for x in (velocity, viscosity, records_t, owner, cell, wall_slot)))


def conduct(t):
    rows = iota(t.shape, 0)
    cols = iota(t.shape, 1)
    for repeat in range(2):
        up = jnp.where(rows == 0, t, pltpu.roll(t, 1, 0))
        down = jnp.where(rows == t.shape[0] - 1, t, pltpu.roll(t, t.shape[0] - 1, 0))
        left = jnp.where(cols == 0, t, pltpu.roll(t, 1, 1))
        right = jnp.where(cols == t.shape[1] - 1, t, pltpu.roll(t, t.shape[1] - 1, 1))
        t = t + COND_STEP * ((down + up + right + left) - 4.0 * t)
    return t


def flow_kernel(where, vel, visc, north, south, west, east, flow_out, field):
    pi, si = where[0], where[1]
    row, col = iota((136, 384), 0), iota((136, 384), 1)
    outside = (
        ((pi == 0) & (row >= 132))
        | ((pi == 15) & (row >= 128) & (row < 132))
        | ((si == 0) & (col >= 320))
        | ((si == 7) & (col >= 256) & (col < 320))
    )
    west_cells, east_cells = west[...].T, east[...].T
    for c in range(4):
        field[c, :, 256:384] = jnp.zeros((136, 128), F32)
        field[c, 128:136, 0:256] = jnp.zeros((8, 256), F32)
        field[c, 0:128, 0:256] = vel[c] if c < 3 else visc[...]
        field[c, 134:136, 0:256] = north[2 * c : 2 * c + 2, :]
        field[c, 128:130, 0:256] = south[2 * c : 2 * c + 2, :]
        field[c, 0:128, 382:384] = west_cells[:, 2 * c : 2 * c + 2]
        field[c, 0:128, 256:258] = east_cells[:, 2 * c : 2 * c + 2]
    nu = field[3]
    faces = []
    for axis, size in ((1, 384), (0, 136)):
        for shift in (size - 1, 1):
            faces.append((0.5 * (pltpu.roll(nu, shift, axis) + nu), shift, axis))
    for c in range(3):
        f = field[c]
        for sweep in range(2):
            flux = jnp.zeros_like(f)
            for face, shift, axis in faces:
                flux = flux + face * (pltpu.roll(f, shift, axis) - f)
            f = f + FLOW_STEP * flux
            if sweep == 0:
                f = jnp.where(outside, 0.0, f)
        flow_out[c] = f[0:128, 0:256]


def flow_call(where, velocity, viscosity, halos):
    return pl.pallas_call(
        flow_kernel,
        out_shape=pltpu.HBM((3, 128, 256), F32),
        in_specs=[pl.BlockSpec(memory_space=pltpu.SMEM)] + [pl.BlockSpec(memory_space=pltpu.VMEM)] * 6,
        out_specs=pl.BlockSpec(memory_space=pltpu.VMEM),
        scratch_shapes=[pltpu.VMEM((4, 136, 384), F32)],
        compiler_params=pltpu.CompilerParams(vmem_limit_bytes=16 << 20),
        name="flow",
    )(where, velocity, viscosity, *halos)


def corner_parts(where, got, visc, north, south, west, east):
    pi, si = where[0], where[1]
    row, lane = iota((8, 128), 0), iota((8, 128), 1)
    parts = []
    for down in range(2):
        for over in range(2):
            there_p = pi + 2 * down - 1
            there_s = si + 2 * over - 1
            inside = (there_p >= 0) & (there_p < 16) & (there_s >= 0) & (there_s < 8)
            source = jnp.where(inside, there_p * 8 + there_s, 0)
            cells = got[pl.ds(source * ROWS + 19 - down, 1), :]
            cells = jnp.broadcast_to(jnp.where(inside, cells, 0.0), (8, 128))
            cells = jnp.where(lane == LIST + 4 * (1 - over) + row, cells, 0.0)
            far = jnp.sum(cells, axis=1, keepdims=True)[0:4]
            beside = [
                jnp.concatenate([ref[2 * c + k : 2 * c + k + 1, at : at + 1] for c in range(4)], axis=0)
                for ref, k, at in (
                    (south if down else north, 1 - down, 255 * over),
                    (east if over else west, 1 - over, 127 * down),
                )
            ]
            own_nu = visc[127 * down : 127 * down + 1, 255 * over : 255 * over + 1]
            part = jnp.zeros((4, 1), F32)
            for near in beside:
                nu = near[3:4]
                first = (0.5 * FLOW_STEP) * ((far[3:4] + nu) * (far - near) + nu * near)
                part = part + (0.5 * FLOW_STEP) * (nu + own_nu) * first
            parts.append(part)
    return parts


def receive_kernel(
    where, got, deposit, visc, north, south, west, east, flow_in,
    arrived_h, deposit_out, flow_h, most, h1_ref, h2_ref, h1_low, h2_low, acc, acc_low, arrived, tiles, sems,
):
    places = [(pl.ds(120 * down, 8), pl.ds(128 * over, 128)) for down in range(2) for over in range(2)]
    loads = [
        pltpu.make_async_copy(flow_in.at[:, rows, cols], tiles.at[i], sems.at[1 + i])
        for i, (rows, cols) in enumerate(places)
    ]
    for load in loads:
        load.start()
    lane = iota((8, 128), 1)
    wide = iota((64, 128), 1)
    even = ((wide >= 32) & (wide < 36)) | ((wide >= 96) & (wide < 100))
    odd = ((wide >= 64) & (wide < 68)) | (wide < 4)
    upto = iota((256, 128), 0).astype(F32).astype(BF16)

    groups = DEVICES // 16

    def stack(row):
        return jnp.concatenate([got[pl.ds(row + g * (16 * ROWS), 8), :] for g in range(groups)], axis=0)

    def fan(row):
        one = [got[pl.ds(row + g * (16 * ROWS), 1), :] for g in range(groups)]
        return jnp.concatenate(
            [pltpu.roll(jnp.broadcast_to(x, (8, 128)), 4, 1, stride=4, stride_axis=0) for x in one], axis=0
        )

    def unpack(s, carry):
        at = s * CAP
        tile, off = at >> 7, at & 127
        halves = []
        for h in range(2):
            body = stack(s * ROWS + 8 * h)
            rest = fan(s * ROWS + 16 + h)
            halves.append((jnp.where(even, rest, body), jnp.where(odd, rest, body)))
        for k in range(4):
            last = pltpu.roll(halves[1][k % 2], HALF, 1)
            piece = jnp.where((wide >= 32 * k) & (wide < 32 * k + HALF) | (wide < 32 * k + HALF - 128), halves[0][k % 2], last)
            piece = pltpu.roll(piece, (at - 32 * k) & 127, 1)
            over = off + CAP > 128
            for g in range(groups):
                mine = piece[8 * g : 8 * g + 8]
                to = pl.ds(pl.multiple_of((g * 9 + tile) * 128, 128), 128)
                made = jnp.where(lane >= off, mine, arrived[8 * k : 8 * k + 8, to])
                arrived[8 * k : 8 * k + 8, to] = made
                to = pl.ds(pl.multiple_of((g * 9 + tile + over.astype(I32)) * 128, 128), 128)
                arrived[8 * k : 8 * k + 8, to] = jnp.where(over, mine, made)
        return carry

    def build(g, slot):
        spot16 = got[pl.ds(g * (16 * ROWS) + 18, 16, stride=ROWS), :].astype(I32)
        amount16 = got[pl.ds(g * (16 * ROWS) + 19, 16, stride=ROWS), :]
        amount16 = jnp.where(iota((16, 128), 1) < LIST, amount16, 0.0)
        firsts = (spot16 >> 8).astype(F32)
        seconds = (spot16 & 255).astype(F32)
        highs = amount16.astype(BF16).astype(F32)
        lows = (amount16 - highs) * LIFT
        one = jnp.ones((256, 128), BF16)
        zero = jnp.zeros((256, 128), BF16)
        for s in range(16):
            here = pl.ds(s * 128, 128)
            row = lambda x: jnp.broadcast_to(x[s : s + 1].astype(BF16), (256, 128))
            first = jnp.where(upto == row(firsts), one, zero)
            h1_ref[slot, :, here] = first
            h1_low[slot, :, here] = first.astype(F8)
            same = upto == row(seconds)
            h2_ref[slot, :, here] = jnp.where(same, row(highs), zero)
            h2_low[slot, :, here] = jnp.where(same, row(lows), zero).astype(F8)

    def add(slot):
        acc[...] += lax.dot_general(h1_ref[slot], h2_ref[slot], NT, preferred_element_type=F32)
        acc_low[...] += lax.dot_general(h1_low[slot], h2_low[slot], NT, preferred_element_type=F32)

    acc[...] = jnp.zeros_like(acc)
    acc_low[...] = jnp.zeros_like(acc_low)
    build(0, 0)

    def pair_of_groups(u, carry):
        unpack(4 * u, 0)
        build(2 * u + 1, 1)
        unpack(4 * u + 1, 0)
        add(0)
        unpack(4 * u + 2, 0)
        build(jnp.minimum(2 * u + 2, 7), 0)
        unpack(4 * u + 3, 0)
        add(1)
        return carry

    lax.fori_loop(0, 4, pair_of_groups, 0)
    arrived_copy = pltpu.make_async_copy(arrived, arrived_h, sems.at[0])
    arrived_copy.start()
    for load in loads:
        load.wait()
    parts = corner_parts(where, got, visc, north, south, west, east)
    side_row, side_col = iota((8, 128), 0), iota((8, 128), 1)
    stores = []
    for i, (rows, cols) in enumerate(places):
        here = (side_row == 7 * (i // 2)) & (side_col == 127 * (i % 2))
        for c in range(3):
            tiles[i, c] = tiles[i, c] + jnp.where(here, parts[i][c : c + 1], 0.0)
        stores.append(pltpu.make_async_copy(tiles.at[i], flow_h.at[:, rows, cols], sems.at[5 + i]))
        stores[-1].start()
    struck = acc[...] + acc_low[...] * (1.0 / LIFT)
    struck = jnp.concatenate([struck[64 * c : 64 * c + 64] for c in range(4)], axis=1)
    had = deposit[...]
    deposit_out[...] = conduct(had + jnp.exp(-had) * struck)
    counts = got[pl.ds(18, DEVICES, stride=ROWS), :]
    most[...] = jnp.max(counts[:, 127:], axis=0, keepdims=True).reshape(1, 1)
    for store in stores:
        store.wait()
    arrived_copy.wait()


def receive(where, got, deposit, viscosity, halos, flow):
    return pl.pallas_call(
        receive_kernel,
        out_shape=(
            pltpu.HBM((WIDTH, DEVICES * CAP), F32),
            pltpu.HBM((64, 1024), F32),
            pltpu.HBM((3, 128, 256), F32),
            jax.ShapeDtypeStruct((1, 1), F32),
        ),
        in_specs=[pl.BlockSpec(memory_space=pltpu.SMEM)]
        + [pl.BlockSpec(memory_space=pltpu.VMEM)] * 7
        + [pl.BlockSpec(memory_space=pl.ANY)],
        out_specs=[
            pl.BlockSpec(memory_space=pl.ANY),
            pl.BlockSpec(memory_space=pltpu.VMEM),
            pl.BlockSpec(memory_space=pl.ANY),
            pl.BlockSpec(memory_space=pltpu.VMEM),
        ],
        scratch_shapes=[
            pltpu.VMEM((2, 256, 2048), BF16),
            pltpu.VMEM((2, 256, 2048), BF16),
            pltpu.VMEM((2, 256, 2048), F8),
            pltpu.VMEM((2, 256, 2048), F8),
            pltpu.VMEM((256, 256), F32),
            pltpu.VMEM((256, 256), F32),
            pltpu.VMEM((WIDTH, DEVICES * CAP), F32),
            pltpu.VMEM((4, 3, 8, 128), F32),
            pltpu.SemaphoreType.DMA((9,)),
        ],
        input_output_aliases={8: 2},
        compiler_params=pltpu.CompilerParams(vmem_limit_bytes=48 << 20),
        name="receive",
    )(where, got, deposit, viscosity, *halos, flow)


def shifted(cells, axis, up):
    count = lax.axis_size(axis)
    pairs = [(i, i + 1) if up else (i + 1, i) for i in range(count - 1)]
    return lax.ppermute(cells, axis, pairs)


def conduct_plain(thickness):
    for repeat in range(2):
        padded = jnp.pad(thickness, 1, mode="edge")
        beside = padded[2:, 1:-1] + padded[:-2, 1:-1] + padded[1:-1, 2:] + padded[1:-1, :-2]
        thickness = thickness + COND_STEP * (beside - 4.0 * thickness)
    return thickness


def all_of_lists(aux, deposit, most):
    amount, spot = aux[0], aux[1]
    wall_dev, rank = aux[2].astype(I32), aux[3].astype(I32)

    def one_round(state):
        turn, total = state
        low = turn * LIST
        taken = (rank >= low) & (rank < low + LIST)
        index = jnp.where(taken, wall_dev * 128 + rank - low, DEVICES * 128)
        lists = jnp.zeros((DEVICES * 128, 2), F32)
        lists = lists.at[index].set(jnp.stack([amount, spot], axis=1), mode="drop")
        lists = lists.reshape(DEVICES, 128, 2).transpose(0, 2, 1).reshape(DEVICES, 1, 256)
        lists = lax.all_to_all(lists, ("passage", "span"), 0, 0, tiled=True).reshape(DEVICES, 2, 128)
        code = lists[:, 1].reshape(-1).astype(I32)
        first, second = code >> 8, code & 255
        place = (first & 63) * 1024 + (first >> 6) * 256 + second
        added = jnp.zeros((64 * 1024,), F32).at[place].add(lists[:, 0].reshape(-1))
        return turn + 1, total + added.reshape(64, 1024)

    total = lax.while_loop(lambda state: state[0] * LIST < most.astype(I32), one_round, (0, jnp.zeros((64, 1024), F32)))[1]
    return conduct_plain(deposit + jnp.exp(-deposit) * total)


def local(velocity, viscosity, records, owner, cell, wall_slot, deposit):
    packed, aux, top, bottom, left, right = send(
        velocity, viscosity, records.T, owner.reshape(1, COUNT), cell.reshape(1, COUNT), wall_slot.reshape(1, COUNT)
    )
    got = lax.all_to_all(packed.reshape(DEVICES, 1, ROWS * 128), ("passage", "span"), 0, 0, tiled=True)
    halos = (
        shifted(bottom, "passage", True),
        shifted(top, "passage", False),
        shifted(right, "span", True),
        shifted(left, "span", False),
    )
    where = jnp.stack([lax.axis_index("passage"), lax.axis_index("span")]).astype(I32)
    flow_out = flow_call(where, velocity, viscosity, halos)
    arrived, deposit_out, flow_out, most = receive(
        where, got.reshape(DEVICES * ROWS, 128), deposit, viscosity, halos, flow_out
    )
    most = most[0, 0]
    deposit_out = lax.cond(
        most > LIST, lambda: all_of_lists(aux, deposit, most), lambda: deposit_out
    )
    return flow_out, arrived.T, deposit_out


def solution(mesh):
    each = ("passage", "span")
    tile = P(None, "passage", "span")
    rows = P(each, None)
    return jax.shard_map(
        local,
        mesh=mesh,
        in_specs=(tile, P("passage", "span"), rows, rows, P(each), P(each), rows),
        out_specs=(tile, rows, rows),
        check_vma=False,
    )
```

```python
import functools

import jax
import jax.numpy as jnp
from jax import lax
from jax.experimental import pallas as pl
from jax.experimental.pallas import tpu as pltpu
from jax.sharding import PartitionSpec as P

FLOW_STEP = 0.1
COND_STEP = 0.2
MOVE_STEP = 0.5
DEVICES = 128
COUNT = 8192
WIDTH = 32
CAP = 72
HALF = 36
ROWS = 20
LIST = 119
CHUNK = 1024
BLOCK = 256
NT = (((1,), (1,)), ((), ()))
F32 = jnp.float32
BF16 = jnp.bfloat16
F8 = jnp.float8_e5m2
LIFT = 2.0**20
I32 = jnp.int32


def iota(shape, dim):
    return lax.broadcasted_iota(I32, shape, dim)


def hot(index, size):
    return (iota((size, index.shape[1]), 0) == index).astype(F32)


def split(x):
    high = x.astype(BF16)
    return high, (x - high.astype(F32)).astype(BF16)


def spread(row, size):
    return jnp.broadcast_to(row, (size, row.shape[1]))


def counting(size, lanes):
    return iota((size, lanes), 0).astype(F32).astype(BF16)


def ones_at(row, size):
    here = counting(size, row.shape[1]) == jnp.broadcast_to(row.astype(BF16), (size, row.shape[1]))
    return jnp.where(here, jnp.ones(here.shape, BF16), jnp.zeros(here.shape, BF16))


def send_kernel(
    vel_h, visc_h, rec_h, own_h, cell_h, wall_h, out, aux, top, bottom, left, right,
    vel, rec, own, cell, wall, table, val, meta, a_ref, b_ref, a_low, b_low, a2_ref, b2_ref, acc, acc_low, acc2, base, mix, sems,
):
    copies = [
        pltpu.make_async_copy(source, target, sems.at[i])
        for i, (source, target) in enumerate(
            ((own_h, own), (wall_h, wall), (cell_h, cell), (vel_h, vel.at[0:3]), (visc_h, vel.at[3]), (rec_h, rec))
        )
    ]
    for copy in copies:
        copy.start()
    acc[...] = jnp.zeros_like(acc)
    acc_low[...] = jnp.zeros_like(acc_low)
    acc2[...] = jnp.zeros_like(acc2)
    base[...] = jnp.zeros_like(base)
    earlier = (iota((BLOCK, BLOCK), 0) < iota((BLOCK, BLOCK), 1)).astype(F32).astype(BF16)

    def rank_chunk(t):
        every = []
        for b in range(CHUNK // BLOCK):
            lanes = pl.ds(pl.multiple_of(t * CHUNK + b * BLOCK, BLOCK), BLOCK)
            owner = own[0:1, lanes]
            wall_dev = (owner >> 3) * 8 + (wall[0:1, lanes] >> 16)
            every += [ones_at(owner.astype(F32), 128), ones_at(wall_dev.astype(F32), 128)]
        every = jnp.concatenate(every, axis=0)
        before = jnp.dot(every, earlier, preferred_element_type=F32)
        start = base[...]
        for b in range(CHUNK // BLOCK):
            lanes = pl.ds(pl.multiple_of(t * CHUNK + b * BLOCK, BLOCK), BLOCK)
            both = every[b * 256 : b * 256 + 256].astype(F32)
            picked = both * (before[b * 256 : b * 256 + 256] + jnp.concatenate([start, start], axis=1))
            meta[8:9, lanes] = jnp.sum(picked[:128], axis=0, keepdims=True)
            meta[9:10, lanes] = jnp.sum(picked[128:], axis=0, keepdims=True)
            start = start + jnp.sum(both, axis=1, keepdims=True)
        base[...] = start

    def prepare(i):
        if 1:
            lanes = pl.ds(pl.multiple_of(i * BLOCK, BLOCK), BLOCK)
            owner = own[0:1, lanes]
            place = cell[0:1, lanes]
            slot = wall[0:1, lanes]
            wall_dev = (owner >> 3) * 8 + (slot >> 16)
            rank = meta[8:9, lanes]
            rank2 = meta[9:10, lanes]
            row_hot = ones_at(((place & 128) + (place >> 8)).astype(F32), 256)
            looked = jnp.dot(table[...], row_hot, preferred_element_type=F32)
            col_is = iota((128, BLOCK), 0) == (place & 127)
            fluid = jnp.concatenate(
                [
                    jnp.sum(
                        jnp.where(
                            col_is,
                            looked[c * 128 : c * 128 + 128] + looked[384 + c * 128 : 512 + c * 128],
                            0.0,
                        ),
                        axis=0,
                        keepdims=True,
                    )
                    for c in range(3)
                ],
                axis=0,
            )
            r = rec[:, lanes]
            old = r[0:3]
            new = old + jax.nn.sigmoid(r[3:4]) * (fluid - old)
            values = jnp.concatenate([new, r[3:6], r[6:9] + MOVE_STEP * new, r[9:]], axis=0)
            energy = jnp.sum(new * new, axis=0, keepdims=True)
            mass = r[5:6]
            soft = jnp.maximum(mass, 0.0) + jnp.log1p(jnp.exp(-jnp.abs(mass)))
            amount = jax.nn.sigmoid(r[4:5]) * soft * energy / (1.0 + energy)
            first = ((slot >> 8) & 3) * 64 + ((slot >> 10) & 63)
            second = slot & 255
            aux[0:1, lanes] = amount
            aux[1:2, lanes] = (first * 256 + second).astype(F32)
            aux[2:3, lanes] = wall_dev.astype(F32)
            aux[3:4, lanes] = rank2

            highs = values.astype(BF16).astype(F32)
            val[0:32, lanes] = highs
            val[32:64, lanes] = (values - highs) * LIFT
            late = rank >= HALF
            late2 = rank2 >= 64.0
            high = amount.astype(BF16).astype(F32)
            meta[0:1, lanes] = jnp.where(late, rank - HALF, rank)
            meta[1:2, lanes] = owner.astype(F32) + jnp.where(late, 128.0, 0.0)
            meta[2:3, lanes] = jnp.where(rank2 < LIST, jnp.where(late2, rank2 - 64.0, rank2), 64.0)
            meta[3:4, lanes] = wall_dev.astype(F32) + jnp.where(late2, 128.0, 0.0)
            meta[4:5, lanes] = first.astype(F32)
            meta[5:6, lanes] = second.astype(F32)
            meta[6:7, lanes] = high
            meta[7:8, lanes] = amount - high

    def place_hot(t):
        lanes = pl.ds(pl.multiple_of(t * CHUNK, CHUNK), CHUNK)
        hot_owner = ones_at(meta[1:2, lanes], 256)
        b_ref[...] = hot_owner
        b_low[...] = hot_owner.astype(F8)

    def place_part(t, part, target):
        lanes = pl.ds(pl.multiple_of(t * CHUNK, CHUNK), CHUNK)
        row = lambda ref, i, size: jnp.broadcast_to(ref[i : i + 1, lanes].astype(BF16), (size, CHUNK))
        step = row(meta, 0, 32)
        zero = jnp.zeros((32, CHUNK), BF16)
        main = counting(32, CHUNK) == step
        for f in range(WIDTH):
            to = (f % 8 * 4 + f // 8) * 32
            target[pl.ds(to, 32), :] = jnp.where(main, row(val, part * 32 + f, 32), zero).astype(target.dtype)
        whole = val[part * 32 : part * 32 + 32, lanes].astype(BF16)
        for e in range(4):
            target[pl.ds(1024 + e * 32, 32), :] = jnp.where(step == 32 + e, whole, zero).astype(target.dtype)

    def place_wall(t):
        lanes = pl.ds(pl.multiple_of(t * CHUNK, CHUNK), CHUNK)
        row = lambda ref, i, size: jnp.broadcast_to(ref[i : i + 1, lanes].astype(BF16), (size, CHUNK))
        main = counting(64, CHUNK) == row(meta, 2, 64)
        zero = jnp.zeros((64, CHUNK), BF16)
        b2_ref[...] = ones_at(meta[3:4, lanes], 256)
        for v in range(4):
            a2_ref[pl.ds(v * 64, 64), :] = jnp.where(main, row(meta, 4 + v, 64), zero)

    pieces = CHUNK // BLOCK

    def add(total, left_ref, right_ref):
        total[...] += lax.dot_general(left_ref[...], right_ref[...], NT, preferred_element_type=F32)

    def first_blocks(i, carry):
        prepare(i)
        return carry

    for copy in copies[:3]:
        copy.wait()
    rank_chunk(0)
    for copy in copies[3:5]:
        copy.wait()
    for c in range(4):
        turned = vel[c].T
        left[2 * c : 2 * c + 2, :] = turned[0:2]
        right[2 * c : 2 * c + 2, :] = turned[254:256]
        top[2 * c : 2 * c + 2, :] = vel[c, 0:2, :]
        bottom[2 * c : 2 * c + 2, :] = vel[c, 126:128, :]
        if c < 3:
            for part, x in enumerate(split(turned)):
                for half in range(2):
                    to = pl.ds(part * 384 + c * 128, 128)
                    table[to, half * 128 : half * 128 + 128] = x[half * 128 : half * 128 + 128]
    copies[5].wait()
    for i in range(pieces):
        prepare(i)

    def chunk(t, ahead):
        place_hot(t)
        place_part(t, 0, a_ref)
        place_part(t, 1, a_low)
        place_wall(t)
        add(acc, a_ref, b_ref)
        if ahead:
            rank_chunk(t + 1)
            prepare((t + 1) * pieces)
        add(acc_low, a_low, b_low)
        if ahead:
            prepare((t + 1) * pieces + 1)
        add(acc2, a2_ref, b2_ref)
        if ahead:
            for piece in range(2, pieces):
                prepare((t + 1) * pieces + piece)

    def with_next(t, carry):
        chunk(t, True)
        return carry

    lax.fori_loop(0, COUNT // CHUNK - 1, with_next, 0)
    chunk(COUNT // CHUNK - 1, False)

    def summed(c):
        low = pl.multiple_of(c * 128, 128)
        return acc[pl.ds(low, 128), :] + acc_low[pl.ds(low, 128), :] * (1.0 / LIFT)

    def main_rows(c, carry):
        both = summed(c)
        for h in range(2):
            out[pl.ds(h * 8 + c, 128, stride=ROWS), :] = both[:, h * 128 : (h + 1) * 128].T
        return carry

    lax.fori_loop(0, 8, main_rows, 0)
    rest = summed(8)
    for h in range(2):
        mix[h] = rest[:, h * 128 : (h + 1) * 128]
    for f in range(WIDTH):
        to = 4 * (f // 8 * 8 + 7 - f % 8)
        for h in range(2):
            mix[2 + h, to : to + 4, :] = mix[h, pl.ds(f, 4, stride=32), :]
    for h in range(2):
        out[pl.ds(16 + h, 128, stride=ROWS), :] = mix[2 + h].T
    spot = acc2[0:64, :] * 256.0 + acc2[64:128, :]
    amount = acc2[128:192, :] + acc2[192:256, :]
    spot = jnp.concatenate([spot[:, :128], spot[:, 128:]], axis=0).T
    amount = jnp.concatenate([amount[:, :128], amount[:, 128:]], axis=0).T
    most = jnp.max(base[128:, :])
    lane = iota((128, 128), 1)

    def with_corners(x, row):
        for side in range(2):
            for c in range(4):
                cell_of = vel[c, row : row + 1, 255 * side : 255 * side + 1]
                x = jnp.where(lane == LIST + 4 * side + c, cell_of, x)
        return x

    out[pl.ds(18, 128, stride=ROWS), :] = jnp.where(lane == 127, most, with_corners(spot, 0))
    out[pl.ds(19, 128, stride=ROWS), :] = with_corners(amount, 127)


def send(velocity, viscosity, records_t, owner, cell, wall_slot):
    return pl.pallas_call(
        send_kernel,
        out_shape=(
            jax.ShapeDtypeStruct((DEVICES * ROWS, 128), F32),
            jax.ShapeDtypeStruct((4, COUNT), F32),
            jax.ShapeDtypeStruct((8, 256), F32),
            jax.ShapeDtypeStruct((8, 256), F32),
            jax.ShapeDtypeStruct((8, 128), F32),
            jax.ShapeDtypeStruct((8, 128), F32),
        ),
        in_specs=[pl.BlockSpec(memory_space=pl.ANY)] * 6,
        out_specs=[pl.BlockSpec(memory_space=pltpu.VMEM)] * 6,
        scratch_shapes=[
            pltpu.VMEM((4, 128, 256), F32),
            pltpu.VMEM((WIDTH, COUNT), F32),
            pltpu.VMEM((1, COUNT), I32),
            pltpu.VMEM((1, COUNT), I32),
            pltpu.VMEM((1, COUNT), I32),
            pltpu.VMEM((768, 256), BF16),
            pltpu.VMEM((64, COUNT), F32),
            pltpu.VMEM((16, COUNT), F32),
            pltpu.VMEM((1152, CHUNK), BF16),
            pltpu.VMEM((256, CHUNK), BF16),
            pltpu.VMEM((1152, CHUNK), F8),
            pltpu.VMEM((256, CHUNK), F8),
            pltpu.VMEM((256, CHUNK), BF16),
            pltpu.VMEM((256, CHUNK), BF16),
            pltpu.VMEM((1152, 256), F32),
            pltpu.VMEM((1152, 256), F32),
            pltpu.VMEM((256, 256), F32),
            pltpu.VMEM((256, 128), F32),
            pltpu.VMEM((4, 128, 128), F32),
            pltpu.SemaphoreType.DMA((6,)),
        ],
        compiler_params=pltpu.CompilerParams(vmem_limit_bytes=48 << 20),
        name="send",
    )(*(pltpu.with_memory_space_constraint(x, pltpu.HBM) for x in (velocity, viscosity, records_t, owner, cell, wall_slot)))


def conduct(t):
    rows = iota(t.shape, 0)
    cols = iota(t.shape, 1)
    for repeat in range(2):
        up = jnp.where(rows == 0, t, pltpu.roll(t, 1, 0))
        down = jnp.where(rows == t.shape[0] - 1, t, pltpu.roll(t, t.shape[0] - 1, 0))
        left = jnp.where(cols == 0, t, pltpu.roll(t, 1, 1))
        right = jnp.where(cols == t.shape[1] - 1, t, pltpu.roll(t, t.shape[1] - 1, 1))
        t = t + COND_STEP * ((down + up + right + left) - 4.0 * t)
    return t


def flow_kernel(where, vel, visc, north, south, west, east, flow_out, field):
    pi, si = where[0], where[1]
    row, col = iota((136, 384), 0), iota((136, 384), 1)
    outside = (
        ((pi == 0) & (row >= 132))
        | ((pi == 15) & (row >= 128) & (row < 132))
        | ((si == 0) & (col >= 320))
        | ((si == 7) & (col >= 256) & (col < 320))
    )
    west_cells, east_cells = west[...].T, east[...].T
    for c in range(4):
        field[c, :, 256:384] = jnp.zeros((136, 128), F32)
        field[c, 128:136, 0:256] = jnp.zeros((8, 256), F32)
        field[c, 0:128, 0:256] = vel[c] if c < 3 else visc[...]
        field[c, 134:136, 0:256] = north[2 * c : 2 * c + 2, :]
        field[c, 128:130, 0:256] = south[2 * c : 2 * c + 2, :]
        field[c, 0:128, 382:384] = west_cells[:, 2 * c : 2 * c + 2]
        field[c, 0:128, 256:258] = east_cells[:, 2 * c : 2 * c + 2]
    nu = field[3]
    faces = []
    for axis, size in ((1, 384), (0, 136)):
        for shift in (size - 1, 1):
            faces.append((0.5 * (pltpu.roll(nu, shift, axis) + nu), shift, axis))
    for c in range(3):
        f = field[c]
        for sweep in range(2):
            flux = jnp.zeros_like(f)
            for face, shift, axis in faces:
                flux = flux + face * (pltpu.roll(f, shift, axis) - f)
            f = f + FLOW_STEP * flux
            if sweep == 0:
                f = jnp.where(outside, 0.0, f)
        flow_out[c] = f[0:128, 0:256]


def flow_call(where, velocity, viscosity, halos):
    return pl.pallas_call(
        flow_kernel,
        out_shape=pltpu.HBM((3, 128, 256), F32),
        in_specs=[pl.BlockSpec(memory_space=pltpu.SMEM)] + [pl.BlockSpec(memory_space=pltpu.VMEM)] * 6,
        out_specs=pl.BlockSpec(memory_space=pltpu.VMEM),
        scratch_shapes=[pltpu.VMEM((4, 136, 384), F32)],
        compiler_params=pltpu.CompilerParams(vmem_limit_bytes=16 << 20),
        name="flow",
    )(where, velocity, viscosity, *halos)


def corner_parts(where, got, visc, north, south, west, east):
    pi, si = where[0], where[1]
    row, lane = iota((8, 128), 0), iota((8, 128), 1)
    parts = []
    for down in range(2):
        for over in range(2):
            there_p = pi + 2 * down - 1
            there_s = si + 2 * over - 1
            inside = (there_p >= 0) & (there_p < 16) & (there_s >= 0) & (there_s < 8)
            source = jnp.where(inside, there_p * 8 + there_s, 0)
            cells = got[pl.ds(source * ROWS + 19 - down, 1), :]
            cells = jnp.broadcast_to(jnp.where(inside, cells, 0.0), (8, 128))
            cells = jnp.where(lane == LIST + 4 * (1 - over) + row, cells, 0.0)
            far = jnp.sum(cells, axis=1, keepdims=True)[0:4]
            beside = [
                jnp.concatenate([ref[2 * c + k : 2 * c + k + 1, at : at + 1] for c in range(4)], axis=0)
                for ref, k, at in (
                    (south if down else north, 1 - down, 255 * over),
                    (east if over else west, 1 - over, 127 * down),
                )
            ]
            own_nu = visc[127 * down : 127 * down + 1, 255 * over : 255 * over + 1]
            part = jnp.zeros((4, 1), F32)
            for near in beside:
                nu = near[3:4]
                first = (0.5 * FLOW_STEP) * ((far[3:4] + nu) * (far - near) + nu * near)
                part = part + (0.5 * FLOW_STEP) * (nu + own_nu) * first
            parts.append(part)
    return parts


def receive_kernel(
    where, got, deposit, visc, north, south, west, east, flow_in,
    arrived_h, deposit_out, flow_h, most, h1_ref, h2_ref, h1_low, h2_low, acc, acc_low, arrived, tiles, sems,
):
    places = [(pl.ds(120 * down, 8), pl.ds(128 * over, 128)) for down in range(2) for over in range(2)]
    loads = [
        pltpu.make_async_copy(flow_in.at[:, rows, cols], tiles.at[i], sems.at[1 + i])
        for i, (rows, cols) in enumerate(places)
    ]
    for load in loads:
        load.start()
    lane = iota((8, 128), 1)
    wide = iota((64, 128), 1)
    even = ((wide >= 32) & (wide < 36)) | ((wide >= 96) & (wide < 100))
    odd = ((wide >= 64) & (wide < 68)) | (wide < 4)
    upto = iota((256, 128), 0).astype(F32).astype(BF16)

    groups = DEVICES // 16

    def stack(row):
        return jnp.concatenate([got[pl.ds(row + g * (16 * ROWS), 8), :] for g in range(groups)], axis=0)

    def fan(row):
        one = [got[pl.ds(row + g * (16 * ROWS), 1), :] for g in range(groups)]
        return jnp.concatenate(
            [pltpu.roll(jnp.broadcast_to(x, (8, 128)), 4, 1, stride=4, stride_axis=0) for x in one], axis=0
        )

    def unpack(s, carry):
        at = s * CAP
        tile, off = at >> 7, at & 127
        halves = []
        for h in range(2):
            body = stack(s * ROWS + 8 * h)
            rest = fan(s * ROWS + 16 + h)
            halves.append((jnp.where(even, rest, body), jnp.where(odd, rest, body)))
        for k in range(4):
            last = pltpu.roll(halves[1][k % 2], HALF, 1)
            piece = jnp.where((wide >= 32 * k) & (wide < 32 * k + HALF) | (wide < 32 * k + HALF - 128), halves[0][k % 2], last)
            piece = pltpu.roll(piece, (at - 32 * k) & 127, 1)
            over = off + CAP > 128
            for g in range(groups):
                mine = piece[8 * g : 8 * g + 8]
                to = pl.ds(pl.multiple_of((g * 9 + tile) * 128, 128), 128)
                made = jnp.where(lane >= off, mine, arrived[8 * k : 8 * k + 8, to])
                arrived[8 * k : 8 * k + 8, to] = made
                to = pl.ds(pl.multiple_of((g * 9 + tile + over.astype(I32)) * 128, 128), 128)
                arrived[8 * k : 8 * k + 8, to] = jnp.where(over, mine, made)
        return carry

    def build(g, slot):
        spot16 = got[pl.ds(g * (16 * ROWS) + 18, 16, stride=ROWS), :].astype(I32)
        amount16 = got[pl.ds(g * (16 * ROWS) + 19, 16, stride=ROWS), :]
        amount16 = jnp.where(iota((16, 128), 1) < LIST, amount16, 0.0)
        firsts = (spot16 >> 8).astype(F32)
        seconds = (spot16 & 255).astype(F32)
        highs = amount16.astype(BF16).astype(F32)
        lows = (amount16 - highs) * LIFT
        one = jnp.ones((256, 128), BF16)
        zero = jnp.zeros((256, 128), BF16)
        for s in range(16):
            here = pl.ds(s * 128, 128)
            row = lambda x: jnp.broadcast_to(x[s : s + 1].astype(BF16), (256, 128))
            first = jnp.where(upto == row(firsts), one, zero)
            h1_ref[slot, :, here] = first
            h1_low[slot, :, here] = first.astype(F8)
            same = upto == row(seconds)
            h2_ref[slot, :, here] = jnp.where(same, row(highs), zero)
            h2_low[slot, :, here] = jnp.where(same, row(lows), zero).astype(F8)

    def add(slot):
        acc[...] += lax.dot_general(h1_ref[slot], h2_ref[slot], NT, preferred_element_type=F32)
        acc_low[...] += lax.dot_general(h1_low[slot], h2_low[slot], NT, preferred_element_type=F32)

    acc[...] = jnp.zeros_like(acc)
    acc_low[...] = jnp.zeros_like(acc_low)
    build(0, 0)

    def pair_of_groups(u, carry):
        unpack(4 * u, 0)
        build(2 * u + 1, 1)
        unpack(4 * u + 1, 0)
        add(0)
        unpack(4 * u + 2, 0)
        build(jnp.minimum(2 * u + 2, 7), 0)
        unpack(4 * u + 3, 0)
        add(1)
        return carry

    lax.fori_loop(0, 4, pair_of_groups, 0)
    arrived_copy = pltpu.make_async_copy(arrived, arrived_h, sems.at[0])
    arrived_copy.start()
    for load in loads:
        load.wait()
    parts = corner_parts(where, got, visc, north, south, west, east)
    side_row, side_col = iota((8, 128), 0), iota((8, 128), 1)
    stores = []
    for i, (rows, cols) in enumerate(places):
        here = (side_row == 7 * (i // 2)) & (side_col == 127 * (i % 2))
        for c in range(3):
            tiles[i, c] = tiles[i, c] + jnp.where(here, parts[i][c : c + 1], 0.0)
        stores.append(pltpu.make_async_copy(tiles.at[i], flow_h.at[:, rows, cols], sems.at[5 + i]))
        stores[-1].start()
    struck = acc[...] + acc_low[...] * (1.0 / LIFT)
    struck = jnp.concatenate([struck[64 * c : 64 * c + 64] for c in range(4)], axis=1)
    had = deposit[...]
    deposit_out[...] = conduct(had + jnp.exp(-had) * struck)
    counts = got[pl.ds(18, DEVICES, stride=ROWS), :]
    most[...] = jnp.max(counts[:, 127:], axis=0, keepdims=True).reshape(1, 1)
    for store in stores:
        store.wait()
    arrived_copy.wait()


def receive(where, got, deposit, viscosity, halos, flow):
    return pl.pallas_call(
        receive_kernel,
        out_shape=(
            pltpu.HBM((WIDTH, DEVICES * CAP), F32),
            pltpu.HBM((64, 1024), F32),
            pltpu.HBM((3, 128, 256), F32),
            jax.ShapeDtypeStruct((1, 1), F32),
        ),
        in_specs=[pl.BlockSpec(memory_space=pltpu.SMEM)]
        + [pl.BlockSpec(memory_space=pltpu.VMEM)] * 7
        + [pl.BlockSpec(memory_space=pl.ANY)],
        out_specs=[
            pl.BlockSpec(memory_space=pl.ANY),
            pl.BlockSpec(memory_space=pltpu.VMEM),
            pl.BlockSpec(memory_space=pl.ANY),
            pl.BlockSpec(memory_space=pltpu.VMEM),
        ],
        scratch_shapes=[
            pltpu.VMEM((2, 256, 2048), BF16),
            pltpu.VMEM((2, 256, 2048), BF16),
            pltpu.VMEM((2, 256, 2048), F8),
            pltpu.VMEM((2, 256, 2048), F8),
            pltpu.VMEM((256, 256), F32),
            pltpu.VMEM((256, 256), F32),
            pltpu.VMEM((WIDTH, DEVICES * CAP), F32),
            pltpu.VMEM((4, 3, 8, 128), F32),
            pltpu.SemaphoreType.DMA((9,)),
        ],
        input_output_aliases={8: 2},
        compiler_params=pltpu.CompilerParams(vmem_limit_bytes=48 << 20),
        name="receive",
    )(where, got, deposit, viscosity, *halos, flow)


def shifted(cells, axis, up):
    count = lax.axis_size(axis)
    pairs = [(i, i + 1) if up else (i + 1, i) for i in range(count - 1)]
    return lax.ppermute(cells, axis, pairs)


def conduct_plain(thickness):
    for repeat in range(2):
        padded = jnp.pad(thickness, 1, mode="edge")
        beside = padded[2:, 1:-1] + padded[:-2, 1:-1] + padded[1:-1, 2:] + padded[1:-1, :-2]
        thickness = thickness + COND_STEP * (beside - 4.0 * thickness)
    return thickness


def all_of_lists(aux, deposit, most):
    amount, spot = aux[0], aux[1]
    wall_dev, rank = aux[2].astype(I32), aux[3].astype(I32)

    def one_round(state):
        turn, total = state
        low = turn * LIST
        taken = (rank >= low) & (rank < low + LIST)
        index = jnp.where(taken, wall_dev * 128 + rank - low, DEVICES * 128)
        lists = jnp.zeros((DEVICES * 128, 2), F32)
        lists = lists.at[index].set(jnp.stack([amount, spot], axis=1), mode="drop")
        lists = lists.reshape(DEVICES, 128, 2).transpose(0, 2, 1).reshape(DEVICES, 1, 256)
        lists = lax.all_to_all(lists, ("passage", "span"), 0, 0, tiled=True).reshape(DEVICES, 2, 128)
        code = lists[:, 1].reshape(-1).astype(I32)
        first, second = code >> 8, code & 255
        place = (first & 63) * 1024 + (first >> 6) * 256 + second
        added = jnp.zeros((64 * 1024,), F32).at[place].add(lists[:, 0].reshape(-1))
        return turn + 1, total + added.reshape(64, 1024)

    total = lax.while_loop(lambda state: state[0] * LIST < most.astype(I32), one_round, (0, jnp.zeros((64, 1024), F32)))[1]
    return conduct_plain(deposit + jnp.exp(-deposit) * total)


def local(velocity, viscosity, records, owner, cell, wall_slot, deposit):
    packed, aux, top, bottom, left, right = send(
        velocity, viscosity, records.T, owner.reshape(1, COUNT), cell.reshape(1, COUNT), wall_slot.reshape(1, COUNT)
    )
    got = lax.all_to_all(packed.reshape(DEVICES, 1, ROWS * 128), ("passage", "span"), 0, 0, tiled=True)
    halos = (
        shifted(bottom, "passage", True),
        shifted(top, "passage", False),
        shifted(right, "span", True),
        shifted(left, "span", False),
    )
    where = jnp.stack([lax.axis_index("passage"), lax.axis_index("span")]).astype(I32)
    flow_out = flow_call(where, velocity, viscosity, halos)
    arrived, deposit_out, flow_out, most = receive(
        where, got.reshape(DEVICES * ROWS, 128), deposit, viscosity, halos, flow_out
    )
    most = most[0, 0]
    deposit_out = lax.cond(
        most > LIST, lambda: all_of_lists(aux, deposit, most), lambda: deposit_out
    )
    return flow_out, arrived.T, deposit_out


def solution(mesh):
    each = ("passage", "span")
    tile = P(None, "passage", "span")
    rows = P(each, None)
    return jax.shard_map(
        local,
        mesh=mesh,
        in_specs=(tile, P("passage", "span"), rows, rows, P(each), P(each), rows),
        out_specs=(tile, rows, rows),
        check_vma=False,
    )
```

```python
import functools

import jax
import jax.numpy as jnp
from jax import lax
from jax.experimental import pallas as pl
from jax.experimental.pallas import tpu as pltpu
from jax.sharding import PartitionSpec as P

FLOW_STEP = 0.1
COND_STEP = 0.2
MOVE_STEP = 0.5
DEVICES = 128
COUNT = 8192
WIDTH = 32
CAP = 72
HALF = 36
ROWS = 20
LIST = 119
CHUNK = 1024
BLOCK = 256
NT = (((1,), (1,)), ((), ()))
F32 = jnp.float32
BF16 = jnp.bfloat16
F8 = jnp.float8_e5m2
LIFT = 2.0**20
I32 = jnp.int32


def iota(shape, dim):
    return lax.broadcasted_iota(I32, shape, dim)


def hot(index, size):
    return (iota((size, index.shape[1]), 0) == index).astype(F32)


def split(x):
    high = x.astype(BF16)
    return high, (x - high.astype(F32)).astype(BF16)


def spread(row, size):
    return jnp.broadcast_to(row, (size, row.shape[1]))


def counting(size, lanes):
    return iota((size, lanes), 0).astype(F32).astype(BF16)


def ones_at(row, size):
    here = counting(size, row.shape[1]) == jnp.broadcast_to(row.astype(BF16), (size, row.shape[1]))
    return jnp.where(here, jnp.ones(here.shape, BF16), jnp.zeros(here.shape, BF16))


def send_kernel(
    vel_h, visc_h, rec_h, own_h, cell_h, wall_h, out, aux, top, bottom, left, right,
    vel, rec, own, cell, wall, table, val, meta, a_ref, b_ref, a_low, b_low, a2_ref, b2_ref, acc, acc_low, acc2, base, mix, sems,
):
    copies = [
        pltpu.make_async_copy(source, target, sems.at[i])
        for i, (source, target) in enumerate(
            ((own_h, own), (wall_h, wall), (cell_h, cell), (vel_h, vel.at[0:3]), (visc_h, vel.at[3]), (rec_h, rec))
        )
    ]
    for copy in copies:
        copy.start()
    acc[...] = jnp.zeros_like(acc)
    acc_low[...] = jnp.zeros_like(acc_low)
    acc2[...] = jnp.zeros_like(acc2)
    base[...] = jnp.zeros_like(base)
    earlier = (iota((BLOCK, BLOCK), 0) < iota((BLOCK, BLOCK), 1)).astype(F32).astype(BF16)

    def rank_chunk(t):
        every = []
        for b in range(CHUNK // BLOCK):
            lanes = pl.ds(pl.multiple_of(t * CHUNK + b * BLOCK, BLOCK), BLOCK)
            owner = own[0:1, lanes]
            wall_dev = (owner >> 3) * 8 + (wall[0:1, lanes] >> 16)
            every += [ones_at(owner.astype(F32), 128), ones_at(wall_dev.astype(F32), 128)]
        every = jnp.concatenate(every, axis=0)
        before = jnp.dot(every, earlier, preferred_element_type=F32)
        start = base[...]
        for b in range(CHUNK // BLOCK):
            lanes = pl.ds(pl.multiple_of(t * CHUNK + b * BLOCK, BLOCK), BLOCK)
            both = every[b * 256 : b * 256 + 256].astype(F32)
            picked = both * (before[b * 256 : b * 256 + 256] + jnp.concatenate([start, start], axis=1))
            meta[8:9, lanes] = jnp.sum(picked[:128], axis=0, keepdims=True)
            meta[9:10, lanes] = jnp.sum(picked[128:], axis=0, keepdims=True)
            start = start + jnp.sum(both, axis=1, keepdims=True)
        base[...] = start

    def prepare(i):
        if 1:
            lanes = pl.ds(pl.multiple_of(i * BLOCK, BLOCK), BLOCK)
            owner = own[0:1, lanes]
            place = cell[0:1, lanes]
            slot = wall[0:1, lanes]
            wall_dev = (owner >> 3) * 8 + (slot >> 16)
            rank = meta[8:9, lanes]
            rank2 = meta[9:10, lanes]
            row_hot = ones_at(((place & 128) + (place >> 8)).astype(F32), 256)
            looked = jnp.dot(table[...], row_hot, preferred_element_type=F32)
            col_is = iota((128, BLOCK), 0) == (place & 127)
            fluid = jnp.concatenate(
                [
                    jnp.sum(
                        jnp.where(
                            col_is,
                            looked[c * 128 : c * 128 + 128] + looked[384 + c * 128 : 512 + c * 128],
                            0.0,
                        ),
                        axis=0,
                        keepdims=True,
                    )
                    for c in range(3)
                ],
                axis=0,
            )
            r = rec[:, lanes]
            old = r[0:3]
            new = old + jax.nn.sigmoid(r[3:4]) * (fluid - old)
            values = jnp.concatenate([new, r[3:6], r[6:9] + MOVE_STEP * new, r[9:]], axis=0)
            energy = jnp.sum(new * new, axis=0, keepdims=True)
            mass = r[5:6]
            soft = jnp.maximum(mass, 0.0) + jnp.log1p(jnp.exp(-jnp.abs(mass)))
            amount = jax.nn.sigmoid(r[4:5]) * soft * energy / (1.0 + energy)
            first = ((slot >> 8) & 3) * 64 + ((slot >> 10) & 63)
            second = slot & 255
            aux[0:1, lanes] = amount
            aux[1:2, lanes] = (first * 256 + second).astype(F32)
            aux[2:3, lanes] = wall_dev.astype(F32)
            aux[3:4, lanes] = rank2

            highs = values.astype(BF16).astype(F32)
            val[0:32, lanes] = highs
            val[32:64, lanes] = (values - highs) * LIFT
            late = rank >= HALF
            late2 = rank2 >= 64.0
            high = amount.astype(BF16).astype(F32)
            meta[0:1, lanes] = jnp.where(late, rank - HALF, rank)
            meta[1:2, lanes] = owner.astype(F32) + jnp.where(late, 128.0, 0.0)
            meta[2:3, lanes] = jnp.where(rank2 < LIST, jnp.where(late2, rank2 - 64.0, rank2), 64.0)
            meta[3:4, lanes] = wall_dev.astype(F32) + jnp.where(late2, 128.0, 0.0)
            meta[4:5, lanes] = first.astype(F32)
            meta[5:6, lanes] = second.astype(F32)
            meta[6:7, lanes] = high
            meta[7:8, lanes] = amount - high

    def place_hot(t):
        lanes = pl.ds(pl.multiple_of(t * CHUNK, CHUNK), CHUNK)
        hot_owner = ones_at(meta[1:2, lanes], 256)
        b_ref[...] = hot_owner
        b_low[...] = hot_owner.astype(F8)

    def place_part(t, part, target):
        lanes = pl.ds(pl.multiple_of(t * CHUNK, CHUNK), CHUNK)
        row = lambda ref, i, size: jnp.broadcast_to(ref[i : i + 1, lanes].astype(BF16), (size, CHUNK))
        step = row(meta, 0, 32)
        zero = jnp.zeros((32, CHUNK), BF16)
        main = counting(32, CHUNK) == step
        for f in range(WIDTH):
            to = (f % 8 * 4 + f // 8) * 32
            target[pl.ds(to, 32), :] = jnp.where(main, row(val, part * 32 + f, 32), zero).astype(target.dtype)
        whole = val[part * 32 : part * 32 + 32, lanes].astype(BF16)
        for e in range(4):
            target[pl.ds(1024 + e * 32, 32), :] = jnp.where(step == 32 + e, whole, zero).astype(target.dtype)

    def place_wall(t):
        lanes = pl.ds(pl.multiple_of(t * CHUNK, CHUNK), CHUNK)
        row = lambda ref, i, size: jnp.broadcast_to(ref[i : i + 1, lanes].astype(BF16), (size, CHUNK))
        main = counting(64, CHUNK) == row(meta, 2, 64)
        zero = jnp.zeros((64, CHUNK), BF16)
        b2_ref[...] = ones_at(meta[3:4, lanes], 256)
        for v in range(4):
            a2_ref[pl.ds(v * 64, 64), :] = jnp.where(main, row(meta, 4 + v, 64), zero)

    pieces = CHUNK // BLOCK

    def add(total, left_ref, right_ref):
        total[...] += lax.dot_general(left_ref[...], right_ref[...], NT, preferred_element_type=F32)

    def first_blocks(i, carry):
        prepare(i)
        return carry

    for copy in copies[:3]:
        copy.wait()
    rank_chunk(0)
    for copy in copies[3:5]:
        copy.wait()
    for c in range(4):
        turned = vel[c].T
        left[2 * c : 2 * c + 2, :] = turned[0:2]
        right[2 * c : 2 * c + 2, :] = turned[254:256]
        top[2 * c : 2 * c + 2, :] = vel[c, 0:2, :]
        bottom[2 * c : 2 * c + 2, :] = vel[c, 126:128, :]
        if c < 3:
            for part, x in enumerate(split(turned)):
                for half in range(2):
                    to = pl.ds(part * 384 + c * 128, 128)
                    table[to, half * 128 : half * 128 + 128] = x[half * 128 : half * 128 + 128]
    copies[5].wait()
    for i in range(pieces):
        prepare(i)

    def chunk(t, ahead):
        place_hot(t)
        place_part(t, 0, a_ref)
        place_part(t, 1, a_low)
        place_wall(t)
        add(acc, a_ref, b_ref)
        if ahead:
            rank_chunk(t + 1)
            prepare((t + 1) * pieces)
        add(acc_low, a_low, b_low)
        if ahead:
            prepare((t + 1) * pieces + 1)
        add(acc2, a2_ref, b2_ref)
        if ahead:
            for piece in range(2, pieces):
                prepare((t + 1) * pieces + piece)

    def with_next(t, carry):
        chunk(t, True)
        return carry

    lax.fori_loop(0, COUNT // CHUNK - 1, with_next, 0)
    chunk(COUNT // CHUNK - 1, False)

    def summed(c):
        low = pl.multiple_of(c * 128, 128)
        return acc[pl.ds(low, 128), :] + acc_low[pl.ds(low, 128), :] * (1.0 / LIFT)

    def main_rows(c, carry):
        both = summed(c)
        for h in range(2):
            out[pl.ds(h * 8 + c, 128, stride=ROWS), :] = both[:, h * 128 : (h + 1) * 128].T
        return carry

    lax.fori_loop(0, 8, main_rows, 0)
    rest = summed(8)
    for h in range(2):
        mix[h] = rest[:, h * 128 : (h + 1) * 128]
    for f in range(WIDTH):
        to = 4 * (f // 8 * 8 + 7 - f % 8)
        for h in range(2):
            mix[2 + h, to : to + 4, :] = mix[h, pl.ds(f, 4, stride=32), :]
    for h in range(2):
        out[pl.ds(16 + h, 128, stride=ROWS), :] = mix[2 + h].T
    spot = acc2[0:64, :] * 256.0 + acc2[64:128, :]
    amount = acc2[128:192, :] + acc2[192:256, :]
    spot = jnp.concatenate([spot[:, :128], spot[:, 128:]], axis=0).T
    amount = jnp.concatenate([amount[:, :128], amount[:, 128:]], axis=0).T
    most = jnp.max(base[128:, :])
    lane = iota((128, 128), 1)

    def with_corners(x, row):
        for side in range(2):
            for c in range(4):
                cell_of = vel[c, row : row + 1, 255 * side : 255 * side + 1]
                x = jnp.where(lane == LIST + 4 * side + c, cell_of, x)
        return x

    out[pl.ds(18, 128, stride=ROWS), :] = jnp.where(lane == 127, most, with_corners(spot, 0))
    out[pl.ds(19, 128, stride=ROWS), :] = with_corners(amount, 127)


def send(velocity, viscosity, records_t, owner, cell, wall_slot):
    return pl.pallas_call(
        send_kernel,
        out_shape=(
            jax.ShapeDtypeStruct((DEVICES * ROWS, 128), F32),
            jax.ShapeDtypeStruct((4, COUNT), F32),
            jax.ShapeDtypeStruct((8, 256), F32),
            jax.ShapeDtypeStruct((8, 256), F32),
            jax.ShapeDtypeStruct((8, 128), F32),
            jax.ShapeDtypeStruct((8, 128), F32),
        ),
        in_specs=[pl.BlockSpec(memory_space=pl.ANY)] * 6,
        out_specs=[pl.BlockSpec(memory_space=pltpu.VMEM)] * 6,
        scratch_shapes=[
            pltpu.VMEM((4, 128, 256), F32),
            pltpu.VMEM((WIDTH, COUNT), F32),
            pltpu.VMEM((1, COUNT), I32),
            pltpu.VMEM((1, COUNT), I32),
            pltpu.VMEM((1, COUNT), I32),
            pltpu.VMEM((768, 256), BF16),
            pltpu.VMEM((64, COUNT), F32),
            pltpu.VMEM((16, COUNT), F32),
            pltpu.VMEM((1152, CHUNK), BF16),
            pltpu.VMEM((256, CHUNK), BF16),
            pltpu.VMEM((1152, CHUNK), F8),
            pltpu.VMEM((256, CHUNK), F8),
            pltpu.VMEM((256, CHUNK), BF16),
            pltpu.VMEM((256, CHUNK), BF16),
            pltpu.VMEM((1152, 256), F32),
            pltpu.VMEM((1152, 256), F32),
            pltpu.VMEM((256, 256), F32),
            pltpu.VMEM((256, 128), F32),
            pltpu.VMEM((4, 128, 128), F32),
            pltpu.SemaphoreType.DMA((6,)),
        ],
        compiler_params=pltpu.CompilerParams(vmem_limit_bytes=48 << 20),
        name="send",
    )(*(pltpu.with_memory_space_constraint(x, pltpu.HBM) for x in (velocity, viscosity, records_t, owner, cell, wall_slot)))


def conduct(t):
    rows = iota(t.shape, 0)
    cols = iota(t.shape, 1)
    for repeat in range(2):
        up = jnp.where(rows == 0, t, pltpu.roll(t, 1, 0))
        down = jnp.where(rows == t.shape[0] - 1, t, pltpu.roll(t, t.shape[0] - 1, 0))
        left = jnp.where(cols == 0, t, pltpu.roll(t, 1, 1))
        right = jnp.where(cols == t.shape[1] - 1, t, pltpu.roll(t, t.shape[1] - 1, 1))
        t = t + COND_STEP * ((down + up + right + left) - 4.0 * t)
    return t


def flow_kernel(where, vel, visc, north, south, west, east, flow_out, field):
    pi, si = where[0], where[1]
    row, col = iota((136, 384), 0), iota((136, 384), 1)
    outside = (
        ((pi == 0) & (row >= 132))
        | ((pi == 15) & (row >= 128) & (row < 132))
        | ((si == 0) & (col >= 320))
        | ((si == 7) & (col >= 256) & (col < 320))
    )
    west_cells, east_cells = west[...].T, east[...].T
    for c in range(4):
        field[c, :, 256:384] = jnp.zeros((136, 128), F32)
        field[c, 128:136, 0:256] = jnp.zeros((8, 256), F32)
        field[c, 0:128, 0:256] = vel[c] if c < 3 else visc[...]
        field[c, 134:136, 0:256] = north[2 * c : 2 * c + 2, :]
        field[c, 128:130, 0:256] = south[2 * c : 2 * c + 2, :]
        field[c, 0:128, 382:384] = west_cells[:, 2 * c : 2 * c + 2]
        field[c, 0:128, 256:258] = east_cells[:, 2 * c : 2 * c + 2]
    nu = field[3]
    faces = []
    for axis, size in ((1, 384), (0, 136)):
        for shift in (size - 1, 1):
            faces.append((0.5 * (pltpu.roll(nu, shift, axis) + nu), shift, axis))
    for c in range(3):
        f = field[c]
        for sweep in range(2):
            flux = jnp.zeros_like(f)
            for face, shift, axis in faces:
                flux = flux + face * (pltpu.roll(f, shift, axis) - f)
            f = f + FLOW_STEP * flux
            if sweep == 0:
                f = jnp.where(outside, 0.0, f)
        flow_out[c] = f[0:128, 0:256]


def flow_call(where, velocity, viscosity, halos):
    return pl.pallas_call(
        flow_kernel,
        out_shape=pltpu.HBM((3, 128, 256), F32),
        in_specs=[pl.BlockSpec(memory_space=pltpu.SMEM)] + [pl.BlockSpec(memory_space=pltpu.VMEM)] * 6,
        out_specs=pl.BlockSpec(memory_space=pltpu.VMEM),
        scratch_shapes=[pltpu.VMEM((4, 136, 384), F32)],
        compiler_params=pltpu.CompilerParams(vmem_limit_bytes=16 << 20),
        name="flow",
    )(where, velocity, viscosity, *halos)


def corner_parts(where, got, visc, north, south, west, east):
    pi, si = where[0], where[1]
    row, lane = iota((8, 128), 0), iota((8, 128), 1)
    parts = []
    for down in range(2):
        for over in range(2):
            there_p = pi + 2 * down - 1
            there_s = si + 2 * over - 1
            inside = (there_p >= 0) & (there_p < 16) & (there_s >= 0) & (there_s < 8)
            source = jnp.where(inside, there_p * 8 + there_s, 0)
            cells = got[pl.ds(source * ROWS + 19 - down, 1), :]
            cells = jnp.broadcast_to(jnp.where(inside, cells, 0.0), (8, 128))
            cells = jnp.where(lane == LIST + 4 * (1 - over) + row, cells, 0.0)
            far = jnp.sum(cells, axis=1, keepdims=True)[0:4]
            beside = [
                jnp.concatenate([ref[2 * c + k : 2 * c + k + 1, at : at + 1] for c in range(4)], axis=0)
                for ref, k, at in (
                    (south if down else north, 1 - down, 255 * over),
                    (east if over else west, 1 - over, 127 * down),
                )
            ]
            own_nu = visc[127 * down : 127 * down + 1, 255 * over : 255 * over + 1]
            part = jnp.zeros((4, 1), F32)
            for near in beside:
                nu = near[3:4]
                first = (0.5 * FLOW_STEP) * ((far[3:4] + nu) * (far - near) + nu * near)
                part = part + (0.5 * FLOW_STEP) * (nu + own_nu) * first
            parts.append(part)
    return parts


def receive_kernel(
    where, got, deposit, visc, north, south, west, east, flow_in,
    arrived_h, deposit_out, flow_h, most, h1_ref, h2_ref, h1_low, h2_low, acc, acc_low, arrived, tiles, sems,
):
    places = [(pl.ds(120 * down, 8), pl.ds(128 * over, 128)) for down in range(2) for over in range(2)]
    loads = [
        pltpu.make_async_copy(flow_in.at[:, rows, cols], tiles.at[i], sems.at[1 + i])
        for i, (rows, cols) in enumerate(places)
    ]
    for load in loads:
        load.start()
    lane = iota((8, 128), 1)
    wide = iota((64, 128), 1)
    even = ((wide >= 32) & (wide < 36)) | ((wide >= 96) & (wide < 100))
    odd = ((wide >= 64) & (wide < 68)) | (wide < 4)
    upto = iota((256, 128), 0).astype(F32).astype(BF16)

    groups = DEVICES // 16

    def stack(row):
        return jnp.concatenate([got[pl.ds(row + g * (16 * ROWS), 8), :] for g in range(groups)], axis=0)

    def fan(row):
        one = [got[pl.ds(row + g * (16 * ROWS), 1), :] for g in range(groups)]
        return jnp.concatenate(
            [pltpu.roll(jnp.broadcast_to(x, (8, 128)), 4, 1, stride=4, stride_axis=0) for x in one], axis=0
        )

    def unpack(s, carry):
        at = s * CAP
        tile, off = at >> 7, at & 127
        halves = []
        for h in range(2):
            body = stack(s * ROWS + 8 * h)
            rest = fan(s * ROWS + 16 + h)
            halves.append((jnp.where(even, rest, body), jnp.where(odd, rest, body)))
        for k in range(4):
            last = pltpu.roll(halves[1][k % 2], HALF, 1)
            piece = jnp.where((wide >= 32 * k) & (wide < 32 * k + HALF) | (wide < 32 * k + HALF - 128), halves[0][k % 2], last)
            piece = pltpu.roll(piece, (at - 32 * k) & 127, 1)
            over = off + CAP > 128
            for g in range(groups):
                mine = piece[8 * g : 8 * g + 8]
                to = pl.ds(pl.multiple_of((g * 9 + tile) * 128, 128), 128)
                made = jnp.where(lane >= off, mine, arrived[8 * k : 8 * k + 8, to])
                arrived[8 * k : 8 * k + 8, to] = made
                to = pl.ds(pl.multiple_of((g * 9 + tile + over.astype(I32)) * 128, 128), 128)
                arrived[8 * k : 8 * k + 8, to] = jnp.where(over, mine, made)
        return carry

    def build(g, slot):
        spot16 = got[pl.ds(g * (16 * ROWS) + 18, 16, stride=ROWS), :].astype(I32)
        amount16 = got[pl.ds(g * (16 * ROWS) + 19, 16, stride=ROWS), :]
        amount16 = jnp.where(iota((16, 128), 1) < LIST, amount16, 0.0)
        firsts = (spot16 >> 8).astype(F32)
        seconds = (spot16 & 255).astype(F32)
        highs = amount16.astype(BF16).astype(F32)
        lows = (amount16 - highs) * LIFT
        one = jnp.ones((256, 128), BF16)
        zero = jnp.zeros((256, 128), BF16)
        for s in range(16):
            here = pl.ds(s * 128, 128)
            row = lambda x: jnp.broadcast_to(x[s : s + 1].astype(BF16), (256, 128))
            first = jnp.where(upto == row(firsts), one, zero)
            h1_ref[slot, :, here] = first
            h1_low[slot, :, here] = first.astype(F8)
            same = upto == row(seconds)
            h2_ref[slot, :, here] = jnp.where(same, row(highs), zero)
            h2_low[slot, :, here] = jnp.where(same, row(lows), zero).astype(F8)

    def add(slot):
        acc[...] += lax.dot_general(h1_ref[slot], h2_ref[slot], NT, preferred_element_type=F32)
        acc_low[...] += lax.dot_general(h1_low[slot], h2_low[slot], NT, preferred_element_type=F32)

    acc[...] = jnp.zeros_like(acc)
    acc_low[...] = jnp.zeros_like(acc_low)
    build(0, 0)

    def pair_of_groups(u, carry):
        unpack(4 * u, 0)
        build(2 * u + 1, 1)
        unpack(4 * u + 1, 0)
        add(0)
        unpack(4 * u + 2, 0)
        build(jnp.minimum(2 * u + 2, 7), 0)
        unpack(4 * u + 3, 0)
        add(1)
        return carry

    lax.fori_loop(0, 4, pair_of_groups, 0, unroll=2)
    arrived_copy = pltpu.make_async_copy(arrived, arrived_h, sems.at[0])
    arrived_copy.start()
    for load in loads:
        load.wait()
    parts = corner_parts(where, got, visc, north, south, west, east)
    side_row, side_col = iota((8, 128), 0), iota((8, 128), 1)
    stores = []
    for i, (rows, cols) in enumerate(places):
        here = (side_row == 7 * (i // 2)) & (side_col == 127 * (i % 2))
        for c in range(3):
            tiles[i, c] = tiles[i, c] + jnp.where(here, parts[i][c : c + 1], 0.0)
        stores.append(pltpu.make_async_copy(tiles.at[i], flow_h.at[:, rows, cols], sems.at[5 + i]))
        stores[-1].start()
    struck = acc[...] + acc_low[...] * (1.0 / LIFT)
    struck = jnp.concatenate([struck[64 * c : 64 * c + 64] for c in range(4)], axis=1)
    had = deposit[...]
    deposit_out[...] = conduct(had + jnp.exp(-had) * struck)
    counts = got[pl.ds(18, DEVICES, stride=ROWS), :]
    most[...] = jnp.max(counts[:, 127:], axis=0, keepdims=True).reshape(1, 1)
    for store in stores:
        store.wait()
    arrived_copy.wait()


def receive(where, got, deposit, viscosity, halos, flow):
    return pl.pallas_call(
        receive_kernel,
        out_shape=(
            pltpu.HBM((WIDTH, DEVICES * CAP), F32),
            pltpu.HBM((64, 1024), F32),
            pltpu.HBM((3, 128, 256), F32),
            jax.ShapeDtypeStruct((1, 1), F32),
        ),
        in_specs=[pl.BlockSpec(memory_space=pltpu.SMEM)]
        + [pl.BlockSpec(memory_space=pltpu.VMEM)] * 7
        + [pl.BlockSpec(memory_space=pl.ANY)],
        out_specs=[
            pl.BlockSpec(memory_space=pl.ANY),
            pl.BlockSpec(memory_space=pltpu.VMEM),
            pl.BlockSpec(memory_space=pl.ANY),
            pl.BlockSpec(memory_space=pltpu.VMEM),
        ],
        scratch_shapes=[
            pltpu.VMEM((2, 256, 2048), BF16),
            pltpu.VMEM((2, 256, 2048), BF16),
            pltpu.VMEM((2, 256, 2048), F8),
            pltpu.VMEM((2, 256, 2048), F8),
            pltpu.VMEM((256, 256), F32),
            pltpu.VMEM((256, 256), F32),
            pltpu.VMEM((WIDTH, DEVICES * CAP), F32),
            pltpu.VMEM((4, 3, 8, 128), F32),
            pltpu.SemaphoreType.DMA((9,)),
        ],
        input_output_aliases={8: 2},
        compiler_params=pltpu.CompilerParams(vmem_limit_bytes=48 << 20),
        name="receive",
    )(where, got, deposit, viscosity, *halos, flow)


def shifted(cells, axis, up):
    count = lax.axis_size(axis)
    pairs = [(i, i + 1) if up else (i + 1, i) for i in range(count - 1)]
    return lax.ppermute(cells, axis, pairs)


def conduct_plain(thickness):
    for repeat in range(2):
        padded = jnp.pad(thickness, 1, mode="edge")
        beside = padded[2:, 1:-1] + padded[:-2, 1:-1] + padded[1:-1, 2:] + padded[1:-1, :-2]
        thickness = thickness + COND_STEP * (beside - 4.0 * thickness)
    return thickness


def all_of_lists(aux, deposit, most):
    amount, spot = aux[0], aux[1]
    wall_dev, rank = aux[2].astype(I32), aux[3].astype(I32)

    def one_round(state):
        turn, total = state
        low = turn * LIST
        taken = (rank >= low) & (rank < low + LIST)
        index = jnp.where(taken, wall_dev * 128 + rank - low, DEVICES * 128)
        lists = jnp.zeros((DEVICES * 128, 2), F32)
        lists = lists.at[index].set(jnp.stack([amount, spot], axis=1), mode="drop")
        lists = lists.reshape(DEVICES, 128, 2).transpose(0, 2, 1).reshape(DEVICES, 1, 256)
        lists = lax.all_to_all(lists, ("passage", "span"), 0, 0, tiled=True).reshape(DEVICES, 2, 128)
        code = lists[:, 1].reshape(-1).astype(I32)
        first, second = code >> 8, code & 255
        place = (first & 63) * 1024 + (first >> 6) * 256 + second
        added = jnp.zeros((64 * 1024,), F32).at[place].add(lists[:, 0].reshape(-1))
        return turn + 1, total + added.reshape(64, 1024)

    total = lax.while_loop(lambda state: state[0] * LIST < most.astype(I32), one_round, (0, jnp.zeros((64, 1024), F32)))[1]
    return conduct_plain(deposit + jnp.exp(-deposit) * total)


def local(velocity, viscosity, records, owner, cell, wall_slot, deposit):
    packed, aux, top, bottom, left, right = send(
        velocity, viscosity, records.T, owner.reshape(1, COUNT), cell.reshape(1, COUNT), wall_slot.reshape(1, COUNT)
    )
    got = lax.all_to_all(packed.reshape(DEVICES, 1, ROWS * 128), ("passage", "span"), 0, 0, tiled=True)
    halos = (
        shifted(bottom, "passage", True),
        shifted(top, "passage", False),
        shifted(right, "span", True),
        shifted(left, "span", False),
    )
    where = jnp.stack([lax.axis_index("passage"), lax.axis_index("span")]).astype(I32)
    flow_out = flow_call(where, velocity, viscosity, halos)
    arrived, deposit_out, flow_out, most = receive(
        where, got.reshape(DEVICES * ROWS, 128), deposit, viscosity, halos, flow_out
    )
    most = most[0, 0]
    deposit_out = lax.cond(
        most > LIST, lambda: all_of_lists(aux, deposit, most), lambda: deposit_out
    )
    return flow_out, arrived.T, deposit_out


def solution(mesh):
    each = ("passage", "span")
    tile = P(None, "passage", "span")
    rows = P(each, None)
    return jax.shard_map(
        local,
        mesh=mesh,
        in_specs=(tile, P("passage", "span"), rows, rows, P(each), P(each), rows),
        out_specs=(tile, rows, rows),
        check_vma=False,
    )
```
